32 devices in a mesh: scene: 2 (over x), space: 8 (over z, y), sub: 2 (over core).
Axes of the slice: x: 2, y: 2, z: 4, core: 2. Of those that a mesh axis runs over, the one named last changes fastest.
Arguments:
- features: bfloat16 [64, 64, 512], P(('scene', 'space', 'sub')), parts along dimension 0, may hold values from -6 to 6
- occupancy: int32 [64, 512], P(('scene', 'space', 'sub')), parts along dimension 0, may hold values 0 or 1
- face_owner: int32 [64, 6, 1], P(('scene', 'space', 'sub')), parts along dimension 0, may hold values from 0 to 15; in each aligned block of 12 rows (0 to 11, 12 to 23, ..., all dimensions but the last counted through in order) at most 2 rows name the same one
- face_slot: int32 [64, 6], P(('scene', 'space', 'sub')), parts along dimension 0, may hold values from 0 to 1
- line_owner: int32 [64, 20, 1], P(('scene', 'space', 'sub')), parts along dimension 0, may hold values from 0 to 15; in each aligned block of 40 rows (0 to 39, 40 to 79, ..., all dimensions but the last counted through in order) at most 4 rows name the same one
- line_slot: int32 [64, 20], P(('scene', 'space', 'sub')), parts along dimension 0, may hold values from 0 to 1
- weight_one: bfloat16 [27, 64, 64], replicated, may hold values from -0.15625 to 0.15625
- weight_two: bfloat16 [27, 64, 64], replicated, may hold values from -0.15625 to 0.15625
- cotangent: bfloat16 [64, 64, 512], P(('scene', 'space', 'sub')), parts along dimension 0, may hold values from -6 to 6
Outputs:
- block_out: bfloat16 [64, 64, 512], P(('scene', 'space', 'sub')), parts along dimension 0
- feature_grad: bfloat16 [64, 64, 512], P(('scene', 'space', 'sub')), parts along dimension 0
- first_grad: float32 [54, 64, 64], P('scene'), parts along dimension 0
- second_grad: float32 [54, 64, 64], P('scene'), parts along dimension 0
The draws below stay inside these ranges and needn't reach their ends.
There are 2 independent parts, one for each index of `scene`. The reference program is written for one: setup_inputs(seed, part) draws one part's arguments, and reference() takes and returns one part's arrays. A program takes and returns all parts, laid end to end along the dimension named above; an argument that names none is the same for every part. Nothing has to cross between parts.
Inputs may be any that keep to these rules, and one draw needn't show every extreme that they name: `face_owner`: owners are numbered along space+sub. Among the 12 entries of one owner's tiles no owner is named more than 2 times, and in some owner's tiles one owner is named exactly 2 times. `line_owner`: owners are numbered along space+sub. Among the 40 entries of one owner's tiles no owner is named more than 4 times, and in some owner's tiles one owner is named exactly 4 times.
All inputs are finite; a program needn't handle non-finite values. No bound on the sum of `occupancy` on one device may be relied on, other than what follows from the above.
Results may differ from the reference program's by a relative error of at most 0.0032.
Values may be sent and summed in bfloat16 or wider, within the bound.
A program may use at most 128 MiB of HBM per device.

```python
import math
import jax
import jax.numpy as jnp
import numpy as np
from jax import lax

C = 64
TILES_DEV = 2
OWNERS = 16
TILES = 32
FACE_CAP = 2
LINE_CAP = 4
N_SPACE = 8
N_SUB = 2


def with_ends(drawn, own_key, smallest, top_value):
    dims = drawn.shape
    spot = [jax.random.randint(jax.random.fold_in(own_key, axis), (), 0, dims[axis]) for axis in range(len(dims))]
    drawn = drawn.at[tuple(spot)].set(smallest)
    longest = dims.index(max(dims))
    spot[longest] = (spot[longest] + 1) % dims[longest]
    return drawn.at[tuple(spot)].set(top_value)


def levels(rng, shape, cuts, least, largest):
    factor_of = 1.0
    for axis_at, blocks in cuts:
        steps = jax.random.uniform(jax.random.fold_in(jax.random.fold_in(rng, 6), axis_at), (blocks,), jnp.float32, least / len(cuts), largest / len(cuts))
        factor_of = factor_of * jnp.repeat(jnp.exp(steps), shape[axis_at] // blocks).reshape((-1,) + (1,) * (len(shape) - 1 - axis_at))
    return factor_of


def assign_block(stream_key, own, number, rows, count, top, most, slope):
    sequence = jax.random.permutation(stream_key, count)
    crowded, ordinary = shares(count, rows * top, most, slope, True), shares(count, rows * top, most, slope, False)
    places = jnp.arange(count)

    def named(sizes, turn):
        used = int((sizes > 0).sum())
        fixed = max(1, used // 4)
        moved = fixed + (places - fixed + turn * (used - fixed)) % max(1, count - fixed)
        return jnp.zeros((count,), jnp.int32).at[sequence[jnp.where(places < fixed, places, moved)]].set(jnp.asarray(sizes, jnp.int32))

    sizes = jnp.where(number % 4 == 0, named(crowded, number // 4), named(ordinary, number - number // 4 - 1))
    mixed = jax.random.permutation(jax.random.fold_in(own, 3), count)
    source_of, taker = mixed[0:count // 2 * 2:2], mixed[1:count // 2 * 2:2]
    margin = jnp.minimum(sizes[source_of] - 1, most - sizes[taker]) // 2
    margin = jnp.where((source_of == sequence[0]) | (taker == sequence[0]) | (sizes[taker] == 0), 0, jnp.maximum(margin, 0))
    moved = jax.random.randint(jax.random.fold_in(own, 4), (count // 2,), 0, 1 << 20) % (margin + 1)
    sizes = sizes.at[source_of].add(-moved).at[taker].add(moved)
    labels = jnp.searchsorted(jnp.cumsum(sizes), jnp.arange(rows * top), side="right").astype(jnp.int32)
    grid = labels.reshape(top, rows).T
    grid = grid[jax.random.permutation(jax.random.fold_in(own, 1), rows)]
    turn = jax.random.randint(jax.random.fold_in(own, 2), (rows, 1), 0, top)
    return jnp.take_along_axis(grid, (jnp.arange(top)[None, :] + turn) % top, axis=1)


def shares(count, total, limit, slope, full):
    weights = [(1 << 20) // math.isqrt(rank ** slope) + 1 for rank in range(1, count + 1)]
    largest = limit if full else min(limit, max(-(-total // count), total * weights[0] // sum(weights)))
    least = 1 if total - largest >= count - 1 else 0
    counts, spare = [largest] + [least] * (count - 1), total - largest - least * (count - 1)
    while spare > 0:
        free = [i for i in range(1, count) if counts[i] < largest] or [i for i in range(1, count) if counts[i] < limit]
        pool, left = sum([weights[i] for i in free]), spare
        for i in free:
            extra = min(limit - counts[i], max(1, left * weights[i] // pool), spare)
            counts[i] = counts[i] + extra
            spare = spare - extra
    return np.array(counts)


def gaussian(key, dims, scale, bound, shards=(), kind=jnp.bfloat16):
    entries = scale * jax.random.normal(key, dims, jnp.float32)
    if shards:
        entries = entries * levels(key, dims, shards, -0.22, 0.18)
    return jnp.clip(entries, -bound, bound).astype(kind)


def setup_inputs(seed: int = 0, part: int = 0) -> dict:
    splits = jax.random.split(jax.random.key(seed), 10)
    own_keys = jax.random.split(jax.random.fold_in(splits[9], part), 10)
    features = gaussian(own_keys[0], (TILES, C, 512), 1.0, 6.0, ((0, 16),))
    occupancy = with_ends((jax.random.randint(own_keys[1], (TILES, 512), 0, 5) < 3).astype(jnp.int32), jax.random.fold_in(own_keys[1], 1), 0, 1)
    face_owner_keys = jax.random.split(jax.random.fold_in(own_keys[2], 1), TILES * 6 // (6 * TILES_DEV))
    face_owner_turns = jax.random.permutation(jax.random.fold_in(own_keys[2], 3), TILES * 6 // (6 * TILES_DEV))
    face_owner = jax.vmap(lambda own, number: assign_block(jax.random.fold_in(own_keys[2], 2), own, number, 6 * TILES_DEV, OWNERS, 1, FACE_CAP, 2))(face_owner_keys, face_owner_turns).reshape((TILES, 6, 1))
    face_slot = with_ends(jax.random.randint(own_keys[3], (TILES, 6), 0, TILES_DEV), jax.random.fold_in(own_keys[3], 1), 0, TILES_DEV - 1).astype(jnp.int32)
    line_owner_keys = jax.random.split(jax.random.fold_in(own_keys[4], 1), TILES * 20 // (20 * TILES_DEV))
    line_owner_turns = jax.random.permutation(jax.random.fold_in(own_keys[4], 3), TILES * 20 // (20 * TILES_DEV))
    line_owner = jax.vmap(lambda own, number: assign_block(jax.random.fold_in(own_keys[4], 2), own, number, 20 * TILES_DEV, OWNERS, 1, LINE_CAP, 2))(line_owner_keys, line_owner_turns).reshape((TILES, 20, 1))
    line_slot = with_ends(jax.random.randint(own_keys[5], (TILES, 20), 0, TILES_DEV), jax.random.fold_in(own_keys[5], 1), 0, TILES_DEV - 1).astype(jnp.int32)
    weight_one = gaussian(splits[6], (27, C, C), (27 * C) ** -0.5, 0.15625)
    weight_two = gaussian(splits[7], (27, C, C), (27 * C) ** -0.5, 0.15625)
    cotangent = gaussian(own_keys[8], (TILES, C, 512), 1.0, 6.0, ((0, 16),))
    return {"features": features, "occupancy": occupancy, "face_owner": face_owner, "face_slot": face_slot, "line_owner": line_owner, "line_slot": line_slot, "weight_one": weight_one, "weight_two": weight_two, "cotangent": cotangent}


def rest_of(main_axis):
    return [axis_id for axis_id in range(3) if axis_id != main_axis]

def source_slot(padded, extra_dirs):
    region = [-1 if spot_c == 0 else 1 if spot_c == 9 else 0 for spot_c in padded]
    inner_c = [spot_c - 1 for spot_c in padded]
    moving = [axis_id for axis_id in range(3) if region[axis_id] != 0]
    if len(moving) == 0:
        return inner_c[0] * 64 + inner_c[1] * 8 + inner_c[2]
    if len(moving) == 1:
        main_axis = moving[0]
        rest_axes = rest_of(main_axis)
        face_id = main_axis * 2 + (1 if region[main_axis] > 0 else 0)
        return 512 + face_id * 64 + inner_c[rest_axes[0]] * 8 + inner_c[rest_axes[1]]
    index_d = extra_dirs.index(tuple(region))
    if len(moving) == 2:
        main_axis = [axis_id for axis_id in range(3) if region[axis_id] == 0][0]
        return 896 + index_d * 8 + inner_c[main_axis]
    return 896 + index_d * 8 + (0 if region[2] > 0 else 7)

def build_tables():
    face_voxels = np.zeros((6, 64), np.int32)
    for face_id in range(6):
        main_axis = face_id // 2
        rest_axes = rest_of(main_axis)
        for first_c in range(8):
            for second_c in range(8):
                coords = [0, 0, 0]
                coords[main_axis] = 7 * (face_id % 2)
                coords[rest_axes[0]] = first_c
                coords[rest_axes[1]] = second_c
                face_voxels[face_id, first_c * 8 + second_c] = coords[0] * 64 + coords[1] * 8 + coords[2]
    line_voxels = np.zeros((12, 8), np.int32)
    for main_axis in range(3):
        rest_axes = rest_of(main_axis)
        for first_b in range(2):
            for second_b in range(2):
                for along_c in range(8):
                    coords = [0, 0, 0]
                    coords[main_axis] = along_c
                    coords[rest_axes[0]] = 7 * first_b
                    coords[rest_axes[1]] = 7 * second_b
                    line_voxels[main_axis * 4 + first_b * 2 + second_b, along_c] = coords[0] * 64 + coords[1] * 8 + coords[2]
    vectors = [(sign_x, sign_y, sign_z) for sign_x in (-1, 0, 1) for sign_y in (-1, 0, 1) for sign_z in (-1, 0, 1)]
    extra_dirs = [vector for vector in vectors if sum((1 for element in vector if element != 0)) == 2]
    extra_dirs = extra_dirs + [vector for vector in vectors if sum((1 for element in vector if element != 0)) == 3]
    line_need = np.zeros(20, np.int32)
    for index_d, vector in enumerate(extra_dirs):
        zero_axes = [axis_id for axis_id in range(3) if vector[axis_id] == 0]
        main_axis = zero_axes[0] if zero_axes else 2
        rest_axes = rest_of(main_axis)
        first_b = 0 if vector[rest_axes[0]] > 0 else 1
        second_b = 0 if vector[rest_axes[1]] > 0 else 1
        line_need[index_d] = main_axis * 4 + first_b * 2 + second_b
    gather_index = np.zeros((27, 512), np.int32)
    spread_index = np.full((27, 1152), 512, np.int32)
    for offset_id, vector in enumerate(vectors):
        for voxel_id in range(512):
            inner_c = [voxel_id // 64, voxel_id // 8 % 8, voxel_id % 8]
            padded = [inner_c[axis_id] + 1 + vector[axis_id] for axis_id in range(3)]
            target = source_slot(padded, extra_dirs)
            gather_index[offset_id, voxel_id] = target
            spread_index[offset_id, target] = voxel_id
    opposite = np.array([1, 0, 3, 2, 5, 4], np.int32)
    return (face_voxels, line_voxels, line_need, opposite, gather_index.reshape(-1), spread_index.reshape(-1))

def cut_pieces(values, face_voxels, line_voxels):
    tile_count, channels = (values.shape[0], values.shape[1])
    face_rows = jnp.take(values, face_voxels.reshape(-1), axis=2).reshape(tile_count, channels, 6, 64)
    face_rows = face_rows.transpose(0, 2, 1, 3).reshape(tile_count * 6, channels * 64)
    line_rows = jnp.take(values, line_voxels.reshape(-1), axis=2).reshape(tile_count, channels, 12, 8)
    line_rows = line_rows.transpose(0, 2, 1, 3).reshape(tile_count * 12, channels * 8)
    return (face_rows, line_rows)

def assemble(values, face_rows, line_rows):
    tile_count, channels = (values.shape[0], values.shape[1])
    near_faces = face_rows.reshape(tile_count, 6, channels, 64).transpose(0, 2, 1, 3).reshape(tile_count, channels, 384)
    near_lines = line_rows.reshape(tile_count, 20, channels, 8).transpose(0, 2, 1, 3).reshape(tile_count, channels, 160)
    padding = jnp.zeros((tile_count, channels, 96), values.dtype)
    return jnp.concatenate([values, near_faces, near_lines, padding], axis=2)

def split_grad(ext_grad):
    tile_count, channels = (ext_grad.shape[0], ext_grad.shape[1])
    own_part = ext_grad[:, :, :512]
    face_part = ext_grad[:, :, 512:896].reshape(tile_count, channels, 6, 64).transpose(0, 2, 1, 3)
    face_part = face_part.reshape(tile_count * 6, channels * 64).astype(jnp.bfloat16)
    line_part = ext_grad[:, :, 896:1056].reshape(tile_count, channels, 20, 8).transpose(0, 2, 1, 3)
    line_part = line_part.reshape(tile_count * 20, channels * 8).astype(jnp.bfloat16)
    return (own_part, face_part, line_part)

def add_pieces(own_part, face_sums, line_sums, face_voxels, line_voxels):
    tile_count, channels = (own_part.shape[0], own_part.shape[1])
    face_back = face_sums.reshape(tile_count, 6, channels, 64).transpose(0, 2, 1, 3).reshape(tile_count, channels, 384)
    line_back = line_sums.reshape(tile_count, 12, channels, 8).transpose(0, 2, 1, 3).reshape(tile_count, channels, 96)
    own_part = own_part.at[:, :, face_voxels.reshape(-1)].add(face_back)
    return own_part.at[:, :, line_voxels.reshape(-1)].add(line_back)

def by_owner(function, operands):
    shaped = tuple((operand.reshape((N_SPACE * N_SUB, TILES_DEV) + operand.shape[1:]) for operand in operands))
    return lax.map(lambda members: function(*members), shaped)

def conv_forward(source, weight, gather_index):

    def one_block(block_src):
        columns = jnp.take(block_src, gather_index, axis=2)
        columns = columns.reshape(block_src.shape[0], block_src.shape[1], 27, 512).astype(jnp.float32)
        return jnp.einsum('koi,bikv->bov', weight.astype(jnp.float32), columns)
    result = by_owner(one_block, (source,))
    return result.reshape(source.shape[0], weight.shape[1], 512)

def weight_term(upstream, source, gather_index):

    def one_block(grad_block, source_block):
        columns = jnp.take(source_block, gather_index, axis=2)
        columns = columns.reshape(source_block.shape[0], source_block.shape[1], 27, 512).astype(jnp.float32)
        return jnp.einsum('bov,bikv->koi', grad_block.astype(jnp.float32), columns)
    return lax.optimization_barrier(jnp.sum(by_owner(one_block, (upstream, source)), axis=0))

def conv_back(upstream, weight, spread_index):
    tile_count, channels = (upstream.shape[0], upstream.shape[1])
    padded = jnp.concatenate([upstream, jnp.zeros((tile_count, channels, 128), upstream.dtype)], axis=2)

    def one_block(block_src):
        columns = jnp.take(block_src, spread_index, axis=2)
        columns = columns.reshape(block_src.shape[0], channels, 27, 1152).astype(jnp.float32)
        return jnp.einsum('koi,bokx->bix', weight.astype(jnp.float32), columns)
    result = by_owner(one_block, (padded,))
    return result.reshape(tile_count, weight.shape[2], 1152)

def reference(features, occupancy, face_owner, face_slot, line_owner, line_slot, weight_one, weight_two, cotangent):
    face_voxels, line_voxels, line_need, opposite, gather_index, spread_index = build_tables()
    tile_count = features.shape[0]
    live_mask = occupancy.astype(features.dtype)[:, None, :]
    live_float = occupancy.astype(jnp.float32)[:, None, :]
    face_source = ((face_owner[:, :, 0] * TILES_DEV + face_slot) * 6 + jnp.asarray(opposite)[None, :]).reshape(-1)
    line_source = ((line_owner[:, :, 0] * TILES_DEV + line_slot) * 12 + jnp.asarray(line_need)[None, :]).reshape(-1)

    def extend(values):
        face_table, line_table = cut_pieces(values, face_voxels, line_voxels)
        return assemble(values, face_table[face_source], line_table[line_source])

    def fold(ext_grad):
        own_part, face_part, line_part = split_grad(ext_grad)
        face_part = lax.optimization_barrier(face_part).astype(jnp.float32)
        line_part = lax.optimization_barrier(line_part).astype(jnp.float32)
        face_sums = jax.ops.segment_sum(face_part, face_source, num_segments=tile_count * 6)
        line_sums = jax.ops.segment_sum(line_part, line_source, num_segments=tile_count * 12)
        return add_pieces(own_part, face_sums, line_sums, face_voxels, line_voxels)
    grad_scale = 1.0 / math.sqrt(512.0 * tile_count)
    masked = features * live_mask
    masked_ext = extend(masked)
    preact = live_float * conv_forward(masked_ext, weight_one, gather_index)
    hidden = jax.nn.silu(preact).astype(jnp.bfloat16)
    hidden_ext = extend(hidden)
    branch = live_float * conv_forward(hidden_ext, weight_two, gather_index)
    block_out = (masked.astype(jnp.float32) + branch).astype(jnp.bfloat16)
    out_grad = cotangent * live_mask
    second_grad = grad_scale * weight_term(out_grad, hidden_ext, gather_index)
    hidden_grad = fold(conv_back(out_grad, weight_two, spread_index))
    logistic = jax.nn.sigmoid(preact)
    act_grad = (hidden_grad * live_float * logistic * (1.0 + preact * (1.0 - logistic))).astype(jnp.bfloat16)
    first_grad = grad_scale * weight_term(act_grad, masked_ext, gather_index)
    feature_sum = fold(conv_back(act_grad, weight_one, spread_index))
    feature_grad = ((cotangent.astype(jnp.float32) + feature_sum) * live_float).astype(jnp.bfloat16)
    return (block_out, feature_grad, first_grad, second_grad)
```

```python
import math

import jax
import jax.numpy as jnp
from jax import lax
from jax.experimental import pallas as pl
from jax.experimental.pallas import tpu as pltpu
from jax.sharding import PartitionSpec as P

F32 = jnp.float32
BF16 = jnp.bfloat16
OWNER_AXES = ("space", "sub")

_VECTORS = [(x, y, z) for x in (-1, 0, 1) for y in (-1, 0, 1) for z in (-1, 0, 1)]
EXTRA = [v for v in _VECTORS if sum(c != 0 for c in v) == 2]
EXTRA = EXTRA + [v for v in _VECTORS if sum(c != 0 for c in v) == 3]
OPPOSITE = (1, 0, 3, 2, 5, 4)


def line_need():
    need = []
    for vector in EXTRA:
        zero = [a for a in range(3) if vector[a] == 0]
        main = zero[0] if zero else 2
        rest = [a for a in range(3) if a != main]
        b1 = 0 if vector[rest[0]] > 0 else 1
        b2 = 0 if vector[rest[1]] > 0 else 1
        need.append(main * 4 + b1 * 2 + b2)
    return need


DEAL = [k for k in range(27) if k % 3 < 2] + [k for k in range(27) if k % 3 == 2]


def cut_pieces(values, tile, faces, lines):
    for f in range(6):
        end = 7 * (f % 2)
        if f // 2 == 0:
            piece = values[end]
        elif f // 2 == 1:
            piece = values[:, end]
        else:
            piece = values[:, :, end, :]
        faces[tile * 6 + f] = piece
    for main in range(3):
        for b1 in range(2):
            for b2 in range(2):
                if main == 2:
                    piece = values[7 * b1, 7 * b2]
                elif main == 1:
                    piece = values[7 * b1, :, 7 * b2, :]
                else:
                    piece = values[:, 7 * b1, 7 * b2, :]
                lines[tile * 12 + main * 4 + b1 * 2 + b2] = piece


def conv_back(up_rows, weight, wide, spread, tile, own, grad_faces, grad_lines):
    c = up_rows.shape[-1]
    cube = up_rows.reshape(8, 8, 8, c)
    for j in range(3):
        wide[2:10, j : j + 8, :, j * c : (j + 1) * c] = cube
    total = None
    for kx in range(3):
        cols = wide[2 - kx : 12 - kx].reshape(800, 4 * c).astype(BF16)
        term = jnp.dot(cols, weight[kx * 4 * c : (kx + 1) * 4 * c, :], preferred_element_type=F32)
        total = term if total is None else total + term
    total = total.reshape(10, 10, 8, 3 * c)
    spread[:, :, 16:24, :] = jnp.zeros((10, 10, 8, c), F32)
    spread[:, :, 8:16, :] = total[:, :, :, :c]
    spread[:, :, 9:17, :] += total[:, :, :, c : 2 * c]
    spread[:, :, 10:18, :] += total[:, :, :, 2 * c :]
    own[tile] = spread[1:9, 1:9, 9:17, :].reshape(64, 8, c)
    for f in range(6):
        end = 9 * (f % 2)
        if f // 2 == 0:
            piece = spread[end, 1:9, 9:17, :]
        elif f // 2 == 1:
            piece = spread[1:9, end, 9:17, :]
        else:
            piece = spread[1:9, 1:9, 8 + end, :]
        grad_faces[tile * 6 + f] = piece
    for e, vector in enumerate(EXTRA):
        px, py, pz = [9 if d > 0 else 0 for d in vector]
        if vector[2] == 0:
            piece = spread[px, py, 9:17, :]
        elif vector[1] == 0:
            piece = spread[px, 1:9, 8 + pz, :]
        elif vector[0] == 0:
            piece = spread[1:9, py, 8 + pz, :]
        else:
            row = spread[px, py, 8 + pz : 9 + pz, :]
            spot = 0 if vector[2] > 0 else 7
            at = lax.broadcasted_iota(jnp.int32, (8, c), 0)
            piece = jnp.where(at == spot, jnp.broadcast_to(row, (8, c)), 0.0)
        grad_lines[tile * 20 + e] = piece


def fill_outgoing(idx, out, faces, lines, grad_faces, grad_lines):
    served_face, served_line, inv_face, inv_line = idx
    owners, fcap = served_face.shape
    lcap = served_line.shape[1]
    c = faces.shape[-1]

    def one(d, carry):
        rows = []
        for s in range(fcap):
            fwd = faces[served_face[d, s]].reshape(64, c)
            back = grad_faces[inv_face[d, s]].reshape(64, c)
            rows.append(jnp.concatenate([fwd, back], axis=1))
        for s in range(lcap):
            fwd = lines[served_line[d, s]]
            back = grad_lines[inv_line[d, s]]
            rows.append(jnp.concatenate([fwd, back], axis=1))
        out[d] = jnp.concatenate(rows, axis=0).astype(BF16)
        return carry

    lax.fori_loop(0, owners, one, 0)


def unpack(arrived, got_faces, got_lines, fcap, lcap):
    owners = arrived.shape[0]

    def one(d, carry):
        block = arrived[d].astype(F32)
        for s in range(fcap):
            got_faces[d * fcap + s] = block[s * 64 : (s + 1) * 64].reshape(8, 8, -1)
        base = fcap * 64
        for s in range(lcap):
            got_lines[d * lcap + s] = block[base + s * 8 : base + (s + 1) * 8]
        return carry

    lax.fori_loop(0, owners, one, 0)


def build_columns(cube, tile, face_pos, line_pos, got_faces, got_lines, block, wide, cols):
    c = cube.shape[-1]
    block[1:9, 1:9, 8:16, :] = cube
    for f in range(6):
        piece = got_faces[face_pos[tile * 6 + f]][:, :, :c]
        end = 9 * (f % 2)
        if f // 2 == 0:
            block[end, 1:9, 8:16, :] = piece
        elif f // 2 == 1:
            block[1:9, end, 8:16, :] = piece
        else:
            block[1:9, 1:9, 7 + end, :] = piece
    for e, vector in enumerate(EXTRA):
        piece = got_lines[line_pos[tile * 20 + e]][:, :c]
        px, py, pz = [9 if d > 0 else 0 for d in vector]
        if vector[2] == 0:
            block[px, py, 8:16, :] = piece
        elif vector[1] == 0:
            block[px, 1:9, 7 + pz, :] = piece
        elif vector[0] == 0:
            block[1:9, py, 7 + pz, :] = piece
        else:
            spot = 0 if vector[2] > 0 else 7
            block[px, py, 7 + pz : 8 + pz, :] = piece[spot : spot + 1]
    for kz in range(3):
        wide[:, :, :, kz * c : (kz + 1) * c] = block[:, :, 7 + kz : 15 + kz, :]
    for kxy in range(9):
        kx, ky = kxy // 3, kxy % 3
        window = wide[kx : kx + 8, ky : ky + 8].reshape(512, 4 * c).astype(BF16)
        cols[tile * 512 : (tile + 1) * 512, kxy * 4 * c : (kxy + 1) * 4 * c] = window


def fold_pieces(idx, got_faces, got_lines, face_sums, line_sums, own, tiles):
    served_face, served_line = idx
    owners, fcap = served_face.shape
    lcap = served_line.shape[1]
    c = own.shape[-1]
    face_sums[...] = jnp.zeros_like(face_sums)
    line_sums[...] = jnp.zeros_like(line_sums)

    def one(d, carry):
        for s in range(fcap):
            to = served_face[d, s]
            face_sums[to] = face_sums[to] + got_faces[d * fcap + s]
        for s in range(lcap):
            to = served_line[d, s]
            line_sums[to] = line_sums[to] + got_lines[d * lcap + s]
        return carry

    lax.fori_loop(0, owners, one, 0)
    for tile in range(tiles):
        for f in range(6):
            piece = face_sums[tile * 6 + f][:, :, c:]
            end = 7 * (f % 2)
            if f // 2 == 0:
                own[tile, end] += piece
            elif f // 2 == 1:
                own[tile, :, end] += piece
            else:
                own[tile, :, :, end, :] += piece
        for main in range(3):
            for b1 in range(2):
                for b2 in range(2):
                    piece = line_sums[tile * 12 + main * 4 + b1 * 2 + b2][:, c:]
                    if main == 2:
                        own[tile, 7 * b1, 7 * b2] += piece
                    elif main == 1:
                        own[tile, 7 * b1, :, 7 * b2, :] += piece
                    else:
                        own[tile, :, 7 * b1, 7 * b2, :] += piece


def deal_term(upstream, cols, terms):
    c = upstream.shape[0]
    term = jnp.dot(upstream, cols[...], preferred_element_type=F32)
    owners = terms.shape[0]
    share = terms.shape[2] // c
    for d in range(owners):
        parts = []
        for k in DEAL[d * share : (d + 1) * share]:
            lane = (k // 3) * 4 * c + (k % 3) * c
            parts.append(term[:, lane : lane + c])
        while len(parts) < share:
            parts.append(jnp.zeros((c, c), F32))
        terms[d] = (parts[0] if share == 1 else jnp.concatenate(parts, axis=1)).astype(BF16)


def first_kernel(sf, sl, vf, vl, feat, occ, cot, wb, out, rows, own,
                 faces, lines, grad_faces, grad_lines, wide, spread):
    tiles, c = feat.shape[0], feat.shape[1]
    wide[...] = jnp.zeros_like(wide)
    grad_faces[tiles * 6] = jnp.zeros((8, 8, c), F32)
    grad_lines[tiles * 20] = jnp.zeros((8, c), F32)
    for t in range(tiles):
        live = occ[t : t + 1, :].astype(F32)
        masked = (feat[t].astype(F32) * live).T
        rows[t] = masked.reshape(64, 8, c)
        cut_pieces(masked.reshape(8, 8, 8, c), t, faces, lines)
        upstream = (cot[t].astype(F32) * live).T
        conv_back(upstream, wb, wide, spread, t, own, grad_faces, grad_lines)
    fill_outgoing((sf, sl, vf, vl), out, faces, lines, grad_faces, grad_lines)


def second_kernel(sf, sl, vf, vl, fp, lp, arrived, rows, own_in, occ, wf, wb,
                  out, hidden_rows, own_out, terms,
                  faces, lines, grad_faces, grad_lines, wide_back, spread,
                  got_faces, got_lines, face_sums, line_sums, block, wide, cols, own):
    tiles, c = rows.shape[0], rows.shape[3]
    fcap, lcap = sf.shape[1], sl.shape[1]
    wide_back[...] = jnp.zeros_like(wide_back)
    wide[:, :, :, 3 * c :] = jnp.zeros((10, 10, 8, c), F32)
    grad_faces[tiles * 6] = jnp.zeros((8, 8, c), F32)
    grad_lines[tiles * 20] = jnp.zeros((8, c), F32)
    unpack(arrived, got_faces, got_lines, fcap, lcap)
    for t in range(tiles):
        own[t] = own_in[t].reshape(8, 8, 8, c)
        build_columns(rows[t].reshape(8, 8, 8, c), t, fp, lp, got_faces, got_lines, block, wide, cols)
    fold_pieces((sf, sl), got_faces, got_lines, face_sums, line_sums, own, tiles)
    conv = lax.dot_general(wf[...], cols[...], (((1,), (1,)), ((), ())), preferred_element_type=F32)
    grads = []
    for t in range(tiles):
        live = occ[t : t + 1, :].astype(F32)
        pre = live * conv[:, t * 512 : (t + 1) * 512]
        logistic = 1.0 / (1.0 + jnp.exp(-pre))
        hidden = (pre * logistic).astype(BF16).astype(F32).T
        hidden_rows[t] = hidden.reshape(64, 8, c)
        cut_pieces(hidden.reshape(8, 8, 8, c), t, faces, lines)
        grad = own[t].reshape(512, c).T
        act = (grad * live * logistic * (1.0 + pre * (1.0 - logistic))).astype(BF16)
        grads.append(act)
        conv_back(act.astype(F32).T, wb, wide_back, spread, t, own_out, grad_faces, grad_lines)
    fill_outgoing((sf, sl, vf, vl), out, faces, lines, grad_faces, grad_lines)
    deal_term(jnp.concatenate(grads, axis=1), cols, terms)


def third_kernel(sf, sl, fp, lp, arrived, hidden_rows, own_in, occ, feat, cot, wf,
                 block_out, feature_grad, terms,
                 got_faces, got_lines, face_sums, line_sums, block, wide, cols, own):
    tiles, c = feat.shape[0], feat.shape[1]
    fcap, lcap = sf.shape[1], sl.shape[1]
    wide[:, :, :, 3 * c :] = jnp.zeros((10, 10, 8, c), F32)
    unpack(arrived, got_faces, got_lines, fcap, lcap)
    grads = []
    for t in range(tiles):
        own[t] = own_in[t].reshape(8, 8, 8, c)
        build_columns(hidden_rows[t].reshape(8, 8, 8, c), t, fp, lp, got_faces, got_lines, block, wide, cols)
        grads.append((cot[t].astype(F32) * occ[t : t + 1, :].astype(F32)).astype(BF16))
    deal_term(jnp.concatenate(grads, axis=1), cols, terms)
    conv = lax.dot_general(wf[...], cols[...], (((1,), (1,)), ((), ())), preferred_element_type=F32)
    fold_pieces((sf, sl), got_faces, got_lines, face_sums, line_sums, own, tiles)
    for t in range(tiles):
        live = occ[t : t + 1, :].astype(F32)
        branch = live * conv[:, t * 512 : (t + 1) * 512]
        block_out[t] = (feat[t].astype(F32) * live + branch).astype(BF16)
        sums = own[t].reshape(512, c).T
        feature_grad[t] = ((cot[t].astype(F32) + sums) * live).astype(BF16)


def forward_weight(weight):
    c = weight.shape[1]
    flat = weight.reshape(9, 3, c, c).transpose(2, 0, 1, 3)
    return jnp.pad(flat, ((0, 0), (0, 0), (0, 1), (0, 0))).reshape(c, 36 * c)


def back_weight(weight):
    c = weight.shape[1]
    flat = weight.reshape(3, 3, 3, c, c).transpose(0, 1, 3, 2, 4)
    flat = jnp.pad(flat, ((0, 0), (0, 1), (0, 0), (0, 0), (0, 0)))
    return flat.reshape(12 * c, 3 * c)


def trade(outgoing):
    return lax.all_to_all(outgoing, OWNER_AXES, split_axis=0, concat_axis=0, tiled=True)


def plan(owner, want, owners, cap):
    count = owner.shape[0]
    at = jnp.arange(count, dtype=jnp.int32)
    earlier = (at[None, :] < at[:, None]) & (owner[None, :] == owner[:, None])
    pos = owner * cap + jnp.sum(earlier.astype(jnp.int32), axis=1)
    hit = pos[None, :] == jnp.arange(owners * cap, dtype=jnp.int32)[:, None]
    ask = jnp.sum(jnp.where(hit, want[None, :], 0), axis=1).reshape(owners, cap)
    inverse = (count - jnp.sum(jnp.where(hit, count - at[None, :], 0), axis=1)).reshape(owners, cap)
    return pos, ask, inverse


def body(features, occupancy, face_owner, face_slot, line_owner, line_slot, weight_one, weight_two, cotangent):
    owners = lax.axis_size(OWNER_AXES)
    tiles, c = features.shape[0], features.shape[1]
    fcap = max(2, 30 * tiles // (4 * owners) + 1)
    lcap = max(2, 100 * tiles // (4 * owners) + 1)
    share = -(-27 // owners)
    height = fcap * 64 + lcap * 8
    opposite = jnp.array(OPPOSITE, jnp.int32)
    need = jnp.array(line_need(), jnp.int32)
    face_pos, face_ask, inv_face = plan(
        face_owner.reshape(-1), (face_slot * 6 + opposite[None, :]).reshape(-1), owners, fcap)
    line_pos, line_ask, inv_line = plan(
        line_owner.reshape(-1), (line_slot * 12 + need[None, :]).reshape(-1), owners, lcap)
    requested = trade(jnp.concatenate([face_ask, line_ask], axis=1))
    served_face, served_line = requested[:, :fcap], requested[:, fcap:]

    wf1, wf2 = forward_weight(weight_one), forward_weight(weight_two)
    wb1, wb2 = back_weight(weight_one), back_weight(weight_two)
    smem = pl.BlockSpec(memory_space=pltpu.SMEM)
    vmem = pl.BlockSpec(memory_space=pltpu.VMEM)
    params = pltpu.CompilerParams(vmem_limit_bytes=56 * 1024 * 1024)
    shape = jax.ShapeDtypeStruct
    table_scratch = [
        pltpu.VMEM((tiles * 6, 8, 8, c), F32),
        pltpu.VMEM((tiles * 12, 8, c), F32),
        pltpu.VMEM((tiles * 6 + 1, 8, 8, c), F32),
        pltpu.VMEM((tiles * 20 + 1, 8, c), F32),
        pltpu.VMEM((12, 10, 8, 4 * c), F32),
        pltpu.VMEM((10, 10, 24, c), F32),
    ]
    got_scratch = [
        pltpu.VMEM((owners * fcap, 8, 8, 2 * c), F32),
        pltpu.VMEM((owners * lcap, 8, 2 * c), F32),
        pltpu.VMEM((tiles * 6, 8, 8, 2 * c), F32),
        pltpu.VMEM((tiles * 12, 8, 2 * c), F32),
        pltpu.VMEM((10, 10, 24, c), F32),
        pltpu.VMEM((10, 10, 8, 4 * c), F32),
        pltpu.VMEM((tiles * 512, 36 * c), BF16),
        pltpu.VMEM((tiles, 8, 8, 8, c), F32),
    ]
    out_block = shape((owners, height, 2 * c), BF16)
    row_block = shape((tiles, 64, 8, c), F32)
    term_block = shape((owners, c, share * c), BF16)
    volume = shape(features.shape, BF16)

    outgoing, rows, hidden_own = pl.pallas_call(
        first_kernel,
        out_shape=(out_block, row_block, row_block),
        in_specs=[smem] * 4 + [vmem] * 4,
        out_specs=(vmem,) * 3,
        scratch_shapes=table_scratch,
        compiler_params=params,
    )(served_face, served_line, inv_face, inv_line, features, occupancy, cotangent, wb2)
    arrived = trade(outgoing)
    outgoing, hidden_rows, feature_own, first_term = pl.pallas_call(
        second_kernel,
        out_shape=(out_block, row_block, row_block, term_block),
        in_specs=[smem] * 6 + [vmem] * 6,
        out_specs=(vmem,) * 4,
        scratch_shapes=table_scratch + got_scratch,
        compiler_params=params,
    )(served_face, served_line, inv_face, inv_line, face_pos, line_pos,
      arrived, rows, hidden_own, occupancy, wf1, wb1)
    arrived = trade(outgoing)
    first_parts = trade(first_term)
    block_out, feature_grad, second_term = pl.pallas_call(
        third_kernel,
        out_shape=(volume, volume, term_block),
        in_specs=[smem] * 4 + [vmem] * 7,
        out_specs=(vmem,) * 3,
        scratch_shapes=got_scratch,
        compiler_params=params,
    )(served_face, served_line, face_pos, line_pos,
      arrived, hidden_rows, feature_own, occupancy, features, cotangent, wf2)
    second_parts = trade(second_term)
    grad_scale = 1.0 / math.sqrt(512.0 * tiles * owners)

    def finish(parts):
        total = (grad_scale * jnp.sum(parts.astype(F32), axis=0)).astype(BF16)
        gathered = trade(jnp.broadcast_to(total[None], (owners,) + total.shape))
        dealt = gathered.reshape(owners, c, share, c).transpose(0, 2, 1, 3).reshape(owners * share, c, c)
        first = dealt[:18].reshape(9, 2, c, c)
        last = dealt[18:27].reshape(9, 1, c, c)
        return jnp.concatenate([first, last], axis=1).reshape(27, c, c).astype(F32)

    return (block_out, feature_grad, finish(first_parts), finish(second_parts))


def solution(mesh):
    split = P(("scene", "space", "sub"), None, None)
    split2 = P(("scene", "space", "sub"), None)
    in_specs = (split, split2, split, split2, split, split2, P(), P(), split)
    out_specs = (split, split, P("scene", None, None), P("scene", None, None))
    return jax.shard_map(body, mesh=mesh, in_specs=in_specs, out_specs=out_specs, check_vma=False)
```

```python
import math

import jax
import jax.numpy as jnp
from jax import lax
from jax.experimental import pallas as pl
from jax.experimental.pallas import tpu as pltpu
from jax.sharding import PartitionSpec as P

F32 = jnp.float32
BF16 = jnp.bfloat16
OWNER_AXES = ("space", "sub")

_VECTORS = [(x, y, z) for x in (-1, 0, 1) for y in (-1, 0, 1) for z in (-1, 0, 1)]
EXTRA = [v for v in _VECTORS if sum(c != 0 for c in v) == 2]
EXTRA = EXTRA + [v for v in _VECTORS if sum(c != 0 for c in v) == 3]
OPPOSITE = (1, 0, 3, 2, 5, 4)


def line_need():
    need = []
    for vector in EXTRA:
        zero = [a for a in range(3) if vector[a] == 0]
        main = zero[0] if zero else 2
        rest = [a for a in range(3) if a != main]
        b1 = 0 if vector[rest[0]] > 0 else 1
        b2 = 0 if vector[rest[1]] > 0 else 1
        need.append(main * 4 + b1 * 2 + b2)
    return need


DEAL = [k for k in range(27) if k % 3 < 2] + [k for k in range(27) if k % 3 == 2]


def cut_pieces(values, tile, faces, lines):
    for f in range(6):
        end = 7 * (f % 2)
        if f // 2 == 0:
            piece = values[end]
        elif f // 2 == 1:
            piece = values[:, end]
        else:
            piece = values[:, :, end, :]
        faces[tile * 6 + f] = piece
    for main in range(3):
        for b1 in range(2):
            for b2 in range(2):
                if main == 2:
                    piece = values[7 * b1, 7 * b2]
                elif main == 1:
                    piece = values[7 * b1, :, 7 * b2, :]
                else:
                    piece = values[:, 7 * b1, 7 * b2, :]
                lines[tile * 12 + main * 4 + b1 * 2 + b2] = piece


def conv_back(up_rows, weight, wide, spread, tile, own, grad_faces, grad_lines):
    c = up_rows.shape[-1]
    cube = up_rows.reshape(8, 8, 8, c)
    for j in range(3):
        wide[2:10, j : j + 8, :, j * c : (j + 1) * c] = cube
    total = None
    for kx in range(3):
        cols = wide[2 - kx : 12 - kx].reshape(800, 4 * c).astype(BF16)
        term = jnp.dot(cols, weight[kx * 4 * c : (kx + 1) * 4 * c, :], preferred_element_type=F32)
        total = term if total is None else total + term
    total = total.reshape(10, 10, 8, 3 * c)
    spread[:, :, 16:24, :] = jnp.zeros((10, 10, 8, c), F32)
    spread[:, :, 8:16, :] = total[:, :, :, :c]
    spread[:, :, 9:17, :] += total[:, :, :, c : 2 * c]
    spread[:, :, 10:18, :] += total[:, :, :, 2 * c :]
    own[tile] = spread[1:9, 1:9, 9:17, :].reshape(64, 8, c)
    for f in range(6):
        end = 9 * (f % 2)
        if f // 2 == 0:
            piece = spread[end, 1:9, 9:17, :]
        elif f // 2 == 1:
            piece = spread[1:9, end, 9:17, :]
        else:
            piece = spread[1:9, 1:9, 8 + end, :]
        grad_faces[tile * 6 + f] = piece
    for e, vector in enumerate(EXTRA):
        px, py, pz = [9 if d > 0 else 0 for d in vector]
        if vector[2] == 0:
            piece = spread[px, py, 9:17, :]
        elif vector[1] == 0:
            piece = spread[px, 1:9, 8 + pz, :]
        elif vector[0] == 0:
            piece = spread[1:9, py, 8 + pz, :]
        else:
            row = spread[px, py, 8 + pz : 9 + pz, :]
            spot = 0 if vector[2] > 0 else 7
            at = lax.broadcasted_iota(jnp.int32, (8, c), 0)
            piece = jnp.where(at == spot, jnp.broadcast_to(row, (8, c)), 0.0)
        grad_lines[tile * 20 + e] = piece


def fill_outgoing(idx, out, faces, lines, grad_faces, grad_lines):
    served_face, served_line, inv_face, inv_line = idx
    owners, fcap = served_face.shape
    lcap = served_line.shape[1]
    c = faces.shape[-1]

    def one(d, carry):
        rows = []
        for s in range(fcap):
            fwd = faces[served_face[d, s]].reshape(64, c)
            back = grad_faces[inv_face[d, s]].reshape(64, c)
            rows.append(jnp.concatenate([fwd, back], axis=1))
        for s in range(lcap):
            fwd = lines[served_line[d, s]]
            back = grad_lines[inv_line[d, s]]
            rows.append(jnp.concatenate([fwd, back], axis=1))
        out[d] = jnp.concatenate(rows, axis=0).astype(BF16)
        return carry

    lax.fori_loop(0, owners, one, 0)


def unpack(arrived, got_faces, got_lines, fcap, lcap):
    owners = arrived.shape[0]

    def one(d, carry):
        block = arrived[d].astype(F32)
        for s in range(fcap):
            got_faces[d * fcap + s] = block[s * 64 : (s + 1) * 64].reshape(8, 8, -1)
        base = fcap * 64
        for s in range(lcap):
            got_lines[d * lcap + s] = block[base + s * 8 : base + (s + 1) * 8]
        return carry

    lax.fori_loop(0, owners, one, 0)


def build_columns(cube, tile, face_pos, line_pos, got_faces, got_lines, block, wide, cols):
    c = cube.shape[-1]
    block[1:9, 1:9, 8:16, :] = cube
    for f in range(6):
        piece = got_faces[face_pos[tile * 6 + f]][:, :, :c]
        end = 9 * (f % 2)
        if f // 2 == 0:
            block[end, 1:9, 8:16, :] = piece
        elif f // 2 == 1:
            block[1:9, end, 8:16, :] = piece
        else:
            block[1:9, 1:9, 7 + end, :] = piece
    for e, vector in enumerate(EXTRA):
        piece = got_lines[line_pos[tile * 20 + e]][:, :c]
        px, py, pz = [9 if d > 0 else 0 for d in vector]
        if vector[2] == 0:
            block[px, py, 8:16, :] = piece
        elif vector[1] == 0:
            block[px, 1:9, 7 + pz, :] = piece
        elif vector[0] == 0:
            block[1:9, py, 7 + pz, :] = piece
        else:
            spot = 0 if vector[2] > 0 else 7
            block[px, py, 7 + pz : 8 + pz, :] = piece[spot : spot + 1]
    for kz in range(3):
        wide[:, :, :, kz * c : (kz + 1) * c] = block[:, :, 7 + kz : 15 + kz, :]
    for kxy in range(9):
        kx, ky = kxy // 3, kxy % 3
        window = wide[kx : kx + 8, ky : ky + 8].reshape(512, 4 * c).astype(BF16)
        cols[tile * 512 : (tile + 1) * 512, kxy * 4 * c : (kxy + 1) * 4 * c] = window


def fold_pieces(idx, got_faces, got_lines, face_sums, line_sums, own, tiles):
    served_face, served_line = idx
    owners, fcap = served_face.shape
    lcap = served_line.shape[1]
    c = own.shape[-1]
    face_sums[...] = jnp.zeros_like(face_sums)
    line_sums[...] = jnp.zeros_like(line_sums)

    def one(d, carry):
        for s in range(fcap):
            to = served_face[d, s]
            face_sums[to] = face_sums[to] + got_faces[d * fcap + s]
        for s in range(lcap):
            to = served_line[d, s]
            line_sums[to] = line_sums[to] + got_lines[d * lcap + s]
        return carry

    lax.fori_loop(0, owners, one, 0)
    for tile in range(tiles):
        for f in range(6):
            piece = face_sums[tile * 6 + f][:, :, c:]
            end = 7 * (f % 2)
            if f // 2 == 0:
                own[tile, end] += piece
            elif f // 2 == 1:
                own[tile, :, end] += piece
            else:
                own[tile, :, :, end, :] += piece
        for main in range(3):
            for b1 in range(2):
                for b2 in range(2):
                    piece = line_sums[tile * 12 + main * 4 + b1 * 2 + b2][:, c:]
                    if main == 2:
                        own[tile, 7 * b1, 7 * b2] += piece
                    elif main == 1:
                        own[tile, 7 * b1, :, 7 * b2, :] += piece
                    else:
                        own[tile, :, 7 * b1, 7 * b2, :] += piece


def deal_term(upstream, cols, terms):
    c = upstream.shape[0]
    term = jnp.dot(upstream, cols[...], preferred_element_type=F32)
    owners = terms.shape[0]
    share = terms.shape[2] // c
    for d in range(owners):
        parts = []
        for k in DEAL[d * share : (d + 1) * share]:
            lane = (k // 3) * 4 * c + (k % 3) * c
            parts.append(term[:, lane : lane + c])
        while len(parts) < share:
            parts.append(jnp.zeros((c, c), F32))
        terms[d] = (parts[0] if share == 1 else jnp.concatenate(parts, axis=1))


def first_kernel(sf, sl, vf, vl, feat, occ, cot, wb, out, rows, own,
                 faces, lines, grad_faces, grad_lines, wide, spread):
    tiles, c = feat.shape[0], feat.shape[1]
    wide[...] = jnp.zeros_like(wide)
    grad_faces[tiles * 6] = jnp.zeros((8, 8, c), F32)
    grad_lines[tiles * 20] = jnp.zeros((8, c), F32)
    for t in range(tiles):
        live = occ[t : t + 1, :].astype(F32)
        masked = (feat[t].astype(F32) * live).T
        rows[t] = masked.reshape(64, 8, c)
        cut_pieces(masked.reshape(8, 8, 8, c), t, faces, lines)
        upstream = (cot[t].astype(F32) * live).T
        conv_back(upstream, wb, wide, spread, t, own, grad_faces, grad_lines)
    fill_outgoing((sf, sl, vf, vl), out, faces, lines, grad_faces, grad_lines)


def second_kernel(sf, sl, vf, vl, fp, lp, arrived, rows, own_in, occ, wf, wb,
                  out, hidden_rows, own_out, terms,
                  faces, lines, grad_faces, grad_lines, wide_back, spread,
                  got_faces, got_lines, face_sums, line_sums, block, wide, cols, own):
    tiles, c = rows.shape[0], rows.shape[3]
    fcap, lcap = sf.shape[1], sl.shape[1]
    wide_back[...] = jnp.zeros_like(wide_back)
    wide[:, :, :, 3 * c :] = jnp.zeros((10, 10, 8, c), F32)
    grad_faces[tiles * 6] = jnp.zeros((8, 8, c), F32)
    grad_lines[tiles * 20] = jnp.zeros((8, c), F32)
    unpack(arrived, got_faces, got_lines, fcap, lcap)
    for t in range(tiles):
        own[t] = own_in[t].reshape(8, 8, 8, c)
        build_columns(rows[t].reshape(8, 8, 8, c), t, fp, lp, got_faces, got_lines, block, wide, cols)
    fold_pieces((sf, sl), got_faces, got_lines, face_sums, line_sums, own, tiles)
    conv = lax.dot_general(wf[...], cols[...], (((1,), (1,)), ((), ())), preferred_element_type=F32)
    grads = []
    for t in range(tiles):
        live = occ[t : t + 1, :].astype(F32)
        pre = live * conv[:, t * 512 : (t + 1) * 512]
        logistic = 1.0 / (1.0 + jnp.exp(-pre))
        hidden = (pre * logistic).astype(BF16).astype(F32).T
        hidden_rows[t] = hidden.reshape(64, 8, c)
        cut_pieces(hidden.reshape(8, 8, 8, c), t, faces, lines)
        grad = own[t].reshape(512, c).T
        act = (grad * live * logistic * (1.0 + pre * (1.0 - logistic))).astype(BF16)
        grads.append(act)
        conv_back(act.astype(F32).T, wb, wide_back, spread, t, own_out, grad_faces, grad_lines)
    fill_outgoing((sf, sl, vf, vl), out, faces, lines, grad_faces, grad_lines)
    deal_term(jnp.concatenate(grads, axis=1), cols, terms)


def third_kernel(sf, sl, fp, lp, arrived, hidden_rows, own_in, occ, feat, cot, wf,
                 block_out, feature_grad, terms,
                 got_faces, got_lines, face_sums, line_sums, block, wide, cols, own):
    tiles, c = feat.shape[0], feat.shape[1]
    fcap, lcap = sf.shape[1], sl.shape[1]
    wide[:, :, :, 3 * c :] = jnp.zeros((10, 10, 8, c), F32)
    unpack(arrived, got_faces, got_lines, fcap, lcap)
    grads = []
    for t in range(tiles):
        own[t] = own_in[t].reshape(8, 8, 8, c)
        build_columns(hidden_rows[t].reshape(8, 8, 8, c), t, fp, lp, got_faces, got_lines, block, wide, cols)
        grads.append((cot[t].astype(F32) * occ[t : t + 1, :].astype(F32)).astype(BF16))
    deal_term(jnp.concatenate(grads, axis=1), cols, terms)
    conv = lax.dot_general(wf[...], cols[...], (((1,), (1,)), ((), ())), preferred_element_type=F32)
    fold_pieces((sf, sl), got_faces, got_lines, face_sums, line_sums, own, tiles)
    for t in range(tiles):
        live = occ[t : t + 1, :].astype(F32)
        branch = live * conv[:, t * 512 : (t + 1) * 512]
        block_out[t] = (feat[t].astype(F32) * live + branch).astype(BF16)
        sums = own[t].reshape(512, c).T
        feature_grad[t] = ((cot[t].astype(F32) + sums) * live).astype(BF16)


def remote(src, dst, send, recv, device):
    return pltpu.make_async_remote_copy(
        src_ref=src, dst_ref=dst, send_sem=send, recv_sem=recv,
        device_id=device, device_id_type=pl.DeviceIdType.MESH)


def exchange_kernel(outgoing, arrived, send, recv, local):
    owners = outgoing.shape[0]
    subs = lax.axis_size("sub")
    me = lax.axis_index("space") * subs + lax.axis_index("sub")

    def place(i):
        peer = lax.rem(me + i, owners)
        return peer, {"space": peer // subs, "sub": lax.rem(peer, subs)}

    barrier = pltpu.get_barrier_semaphore()
    for i in range(1, owners):
        pl.semaphore_signal(barrier, inc=1, device_id=place(i)[1], device_id_type=pl.DeviceIdType.MESH)
    own = pltpu.make_async_copy(outgoing.at[me], arrived.at[me], local)
    own.start()
    pl.semaphore_wait(barrier, owners - 1)
    order = sorted(range(1, owners), key=lambda i: abs(i - owners // 2))
    copies = []
    for i in order:
        peer, device = place(i)
        copy = remote(outgoing.at[peer], arrived.at[me], send.at[i], recv.at[i], device)
        copy.start()
        copies.append(copy)
    own.wait()
    for copy in copies:
        copy.wait()


def exchange(outgoing, number):
    owners = outgoing.shape[0]
    place = pl.BlockSpec(memory_space=pl.ANY)
    return pl.pallas_call(
        exchange_kernel,
        out_shape=jax.ShapeDtypeStruct(outgoing.shape, outgoing.dtype),
        in_specs=[place],
        out_specs=place,
        scratch_shapes=[
            pltpu.SemaphoreType.DMA((owners,)),
            pltpu.SemaphoreType.DMA((owners,)),
            pltpu.SemaphoreType.DMA,
        ],
        compiler_params=pltpu.CompilerParams(collective_id=number, has_side_effects=True),
    )(outgoing)


def reduce_kernel(scale, first, second, first_out, second_out, halves, sums, parts, gathered,
                  half_send, half_recv, part_send, part_recv, gather_send, gather_recv,
                  last_send, last_recv):
    spaces, c = sums.shape[0], sums.shape[2]
    space, sub = lax.axis_index("space"), lax.axis_index("sub")
    other = 1 - sub
    partner = {"space": space, "sub": other}

    def peer(i):
        at = lax.rem(space + i, spaces)
        return at, {"space": at, "sub": sub}

    barrier = pltpu.get_barrier_semaphore()
    pl.semaphore_signal(barrier, inc=1, device_id=partner, device_id_type=pl.DeviceIdType.MESH)
    for i in range(1, spaces):
        pl.semaphore_signal(barrier, inc=1, device_id=peer(i)[1], device_id_type=pl.DeviceIdType.MESH)
    pl.semaphore_wait(barrier, spaces)
    copies = []
    for j, term in enumerate((first, second)):
        copy = remote(term.at[pl.ds(other * spaces, spaces)], halves.at[j],
                      half_send.at[j], half_recv.at[j], partner)
        copy.start()
        copies.append(copy)
    for copy in copies:
        copy.wait()
    for j, term in enumerate((first, second)):
        for s in range(spaces):
            sums[s, j] = (term[sub * spaces + s] + halves[j, s]).astype(BF16)
    order = sorted(range(1, spaces), key=lambda i: abs(i - spaces // 2))
    copies = []
    for i in order:
        at, device = peer(i)
        copy = remote(sums.at[at], parts.at[space], part_send.at[i], part_recv.at[i], device)
        copy.start()
        copies.append(copy)
    parts[space] = sums[space]
    for copy in copies:
        copy.wait()
    total = parts[0].astype(F32)
    for s in range(1, spaces):
        total = total + parts[s].astype(F32)
    gathered[sub, space] = (total * scale).astype(BF16)
    copies = []
    for i in order:
        at, device = peer(i)
        copy = remote(gathered.at[sub, space], gathered.at[sub, space],
                      gather_send.at[i], gather_recv.at[i], device)
        copy.start()
        copies.append(copy)
    for copy in copies:
        copy.wait()
    copy = remote(gathered.at[sub], gathered.at[sub], last_send, last_recv, partner)
    copy.start()
    copy.wait()
    share = gathered.shape[4] // c
    for at, k in enumerate(DEAL):
        owner, lane = at // share, at % share * c
        for j, out in enumerate((first_out, second_out)):
            out[k] = gathered[owner // spaces, owner % spaces, j][:, lane : lane + c].astype(F32)


def reduce_terms(first, second, scale, number):
    subs, spaces = lax.axis_size("sub"), lax.axis_size("space")
    owners, c, width = first.shape
    vmem = pl.BlockSpec(memory_space=pltpu.VMEM)
    dma = pltpu.SemaphoreType.DMA
    return pl.pallas_call(
        lambda *refs: reduce_kernel(scale, *refs),
        out_shape=(jax.ShapeDtypeStruct((27, c, c), F32),) * 2,
        in_specs=[vmem] * 2,
        out_specs=(vmem,) * 2,
        scratch_shapes=[
            pltpu.VMEM((2, spaces, c, width), F32),
            pltpu.VMEM((spaces, 2, c, width), BF16),
            pltpu.VMEM((spaces, 2, c, width), BF16),
            pltpu.VMEM((subs, spaces, 2, c, width), BF16),
            dma((2,)), dma((2,)), dma((spaces,)), dma((spaces,)),
            dma((spaces,)), dma((spaces,)), dma, dma,
        ],
        compiler_params=pltpu.CompilerParams(
            collective_id=number, has_side_effects=True, vmem_limit_bytes=32 * 1024 * 1024),
    )(first, second)


def forward_weight(weight):
    c = weight.shape[1]
    flat = weight.reshape(9, 3, c, c).transpose(2, 0, 1, 3)
    return jnp.pad(flat, ((0, 0), (0, 0), (0, 1), (0, 0))).reshape(c, 36 * c)


def back_weight(weight):
    c = weight.shape[1]
    flat = weight.reshape(3, 3, 3, c, c).transpose(0, 1, 3, 2, 4)
    flat = jnp.pad(flat, ((0, 0), (0, 1), (0, 0), (0, 0), (0, 0)))
    return flat.reshape(12 * c, 3 * c)


def trade(outgoing):
    return lax.all_to_all(outgoing, OWNER_AXES, split_axis=0, concat_axis=0, tiled=True)


def plan(owner, want, owners, cap):
    count = owner.shape[0]
    at = jnp.arange(count, dtype=jnp.int32)
    earlier = (at[None, :] < at[:, None]) & (owner[None, :] == owner[:, None])
    pos = owner * cap + jnp.sum(earlier.astype(jnp.int32), axis=1)
    hit = pos[None, :] == jnp.arange(owners * cap, dtype=jnp.int32)[:, None]
    ask = jnp.sum(jnp.where(hit, want[None, :], 0), axis=1).reshape(owners, cap)
    inverse = (count - jnp.sum(jnp.where(hit, count - at[None, :], 0), axis=1)).reshape(owners, cap)
    return pos, ask, inverse


def body(features, occupancy, face_owner, face_slot, line_owner, line_slot, weight_one, weight_two, cotangent):
    owners = lax.axis_size(OWNER_AXES)
    tiles, c = features.shape[0], features.shape[1]
    fcap = max(2, 30 * tiles // (4 * owners) + 1)
    lcap = max(2, 100 * tiles // (4 * owners) + 1)
    share = -(-27 // owners)
    height = fcap * 64 + lcap * 8
    opposite = jnp.array(OPPOSITE, jnp.int32)
    need = jnp.array(line_need(), jnp.int32)
    face_pos, face_ask, inv_face = plan(
        face_owner.reshape(-1), (face_slot * 6 + opposite[None, :]).reshape(-1), owners, fcap)
    line_pos, line_ask, inv_line = plan(
        line_owner.reshape(-1), (line_slot * 12 + need[None, :]).reshape(-1), owners, lcap)
    requested = trade(jnp.concatenate([face_ask, line_ask], axis=1))
    served_face, served_line = requested[:, :fcap], requested[:, fcap:]

    wf1, wf2 = forward_weight(weight_one), forward_weight(weight_two)
    wb1, wb2 = back_weight(weight_one), back_weight(weight_two)
    smem = pl.BlockSpec(memory_space=pltpu.SMEM)
    vmem = pl.BlockSpec(memory_space=pltpu.VMEM)
    params = pltpu.CompilerParams(vmem_limit_bytes=56 * 1024 * 1024)
    shape = jax.ShapeDtypeStruct
    table_scratch = [
        pltpu.VMEM((tiles * 6, 8, 8, c), F32),
        pltpu.VMEM((tiles * 12, 8, c), F32),
        pltpu.VMEM((tiles * 6 + 1, 8, 8, c), F32),
        pltpu.VMEM((tiles * 20 + 1, 8, c), F32),
        pltpu.VMEM((12, 10, 8, 4 * c), F32),
        pltpu.VMEM((10, 10, 24, c), F32),
    ]
    got_scratch = [
        pltpu.VMEM((owners * fcap, 8, 8, 2 * c), F32),
        pltpu.VMEM((owners * lcap, 8, 2 * c), F32),
        pltpu.VMEM((tiles * 6, 8, 8, 2 * c), F32),
        pltpu.VMEM((tiles * 12, 8, 2 * c), F32),
        pltpu.VMEM((10, 10, 24, c), F32),
        pltpu.VMEM((10, 10, 8, 4 * c), F32),
        pltpu.VMEM((tiles * 512, 36 * c), BF16),
        pltpu.VMEM((tiles, 8, 8, 8, c), F32),
    ]
    out_block = shape((owners, height, 2 * c), BF16)
    row_block = shape((tiles, 64, 8, c), F32)
    term_block = shape((owners, c, share * c), F32)
    volume = shape(features.shape, BF16)

    outgoing, rows, hidden_own = pl.pallas_call(
        first_kernel,
        out_shape=(out_block, row_block, row_block),
        in_specs=[smem] * 4 + [vmem] * 4,
        out_specs=(vmem,) * 3,
        scratch_shapes=table_scratch,
        compiler_params=params,
    )(served_face, served_line, inv_face, inv_line, features, occupancy, cotangent, wb2)
    arrived = exchange(outgoing, 0)
    outgoing, hidden_rows, feature_own, first_term = pl.pallas_call(
        second_kernel,
        out_shape=(out_block, row_block, row_block, term_block),
        in_specs=[smem] * 6 + [vmem] * 6,
        out_specs=(vmem,) * 4,
        scratch_shapes=table_scratch + got_scratch,
        compiler_params=params,
    )(served_face, served_line, inv_face, inv_line, face_pos, line_pos,
      arrived, rows, hidden_own, occupancy, wf1, wb1)
    arrived = exchange(outgoing, 1)
    block_out, feature_grad, second_term = pl.pallas_call(
        third_kernel,
        out_shape=(volume, volume, term_block),
        in_specs=[smem] * 4 + [vmem] * 7,
        out_specs=(vmem,) * 3,
        scratch_shapes=got_scratch,
        compiler_params=params,
    )(served_face, served_line, face_pos, line_pos,
      arrived, hidden_rows, feature_own, occupancy, features, cotangent, wf2)
    grad_scale = 1.0 / math.sqrt(512.0 * tiles * owners)
    first_grad, second_grad = reduce_terms(first_term, second_term, grad_scale, 2)
    return (block_out, feature_grad, first_grad, second_grad)


def solution(mesh):
    split = P(("scene", "space", "sub"), None, None)
    split2 = P(("scene", "space", "sub"), None)
    in_specs = (split, split2, split, split2, split, split2, P(), P(), split)
    out_specs = (split, split, P("scene", None, None), P("scene", None, None))
    return jax.shard_map(body, mesh=mesh, in_specs=in_specs, out_specs=out_specs, check_vma=False)
```

```python
import math

import jax
import jax.numpy as jnp
from jax import lax
from jax.experimental import pallas as pl
from jax.experimental.pallas import tpu as pltpu
from jax.sharding import PartitionSpec as P

F32 = jnp.float32
BF16 = jnp.bfloat16
OWNER_AXES = ("space", "sub")

_VECTORS = [(x, y, z) for x in (-1, 0, 1) for y in (-1, 0, 1) for z in (-1, 0, 1)]
EXTRA = [v for v in _VECTORS if sum(c != 0 for c in v) == 2]
EXTRA = EXTRA + [v for v in _VECTORS if sum(c != 0 for c in v) == 3]
OPPOSITE = (1, 0, 3, 2, 5, 4)


def line_need():
    need = []
    for vector in EXTRA:
        zero = [a for a in range(3) if vector[a] == 0]
        main = zero[0] if zero else 2
        rest = [a for a in range(3) if a != main]
        b1 = 0 if vector[rest[0]] > 0 else 1
        b2 = 0 if vector[rest[1]] > 0 else 1
        need.append(main * 4 + b1 * 2 + b2)
    return need


DEAL = [k for k in range(27) if k % 3 < 2] + [k for k in range(27) if k % 3 == 2]


def cut_pieces(values, tile, faces, lines):
    for f in range(6):
        end = 7 * (f % 2)
        if f // 2 == 0:
            piece = values[end]
        elif f // 2 == 1:
            piece = values[:, end]
        else:
            piece = values[:, :, end, :]
        faces[tile * 6 + f] = piece
    for main in range(3):
        for b1 in range(2):
            for b2 in range(2):
                if main == 2:
                    piece = values[7 * b1, 7 * b2]
                elif main == 1:
                    piece = values[7 * b1, :, 7 * b2, :]
                else:
                    piece = values[:, 7 * b1, 7 * b2, :]
                lines[tile * 12 + main * 4 + b1 * 2 + b2] = piece


def conv_back(up_rows, weight, wide, spread, tile, own, grad_faces, grad_lines):
    c = up_rows.shape[-1]
    cube = up_rows.reshape(8, 8, 8, c)
    for j in range(3):
        wide[2:10, j : j + 8, :, j * c : (j + 1) * c] = cube
    total = None
    for kx in range(3):
        cols = wide[2 - kx : 12 - kx].reshape(800, 4 * c).astype(BF16)
        term = jnp.dot(cols, weight[kx * 4 * c : (kx + 1) * 4 * c, :], preferred_element_type=F32)
        total = term if total is None else total + term
    total = total.reshape(10, 10, 8, 3 * c)
    spread[:, :, 16:24, :] = jnp.zeros((10, 10, 8, c), F32)
    spread[:, :, 8:16, :] = total[:, :, :, :c]
    spread[:, :, 9:17, :] += total[:, :, :, c : 2 * c]
    spread[:, :, 10:18, :] += total[:, :, :, 2 * c :]
    own[tile] = spread[1:9, 1:9, 9:17, :].reshape(64, 8, c)
    for f in range(6):
        end = 9 * (f % 2)
        if f // 2 == 0:
            piece = spread[end, 1:9, 9:17, :]
        elif f // 2 == 1:
            piece = spread[1:9, end, 9:17, :]
        else:
            piece = spread[1:9, 1:9, 8 + end, :]
        grad_faces[tile * 6 + f] = piece
    for e, vector in enumerate(EXTRA):
        px, py, pz = [9 if d > 0 else 0 for d in vector]
        if vector[2] == 0:
            piece = spread[px, py, 9:17, :]
        elif vector[1] == 0:
            piece = spread[px, 1:9, 8 + pz, :]
        elif vector[0] == 0:
            piece = spread[1:9, py, 8 + pz, :]
        else:
            row = spread[px, py, 8 + pz : 9 + pz, :]
            spot = 0 if vector[2] > 0 else 7
            at = lax.broadcasted_iota(jnp.int32, (8, c), 0)
            piece = jnp.where(at == spot, jnp.broadcast_to(row, (8, c)), 0.0)
        grad_lines[tile * 20 + e] = piece


def fill_outgoing(asked, code, fcap, out, faces, lines, grad_faces, grad_lines):
    owners, cap = asked.shape
    c = faces.shape[-1]
    no_face, no_line = grad_faces.shape[0] - 1, grad_lines.shape[0] - 1

    def one(d, carry):
        rows = []
        for s in range(cap):
            want = asked[d, s] & 63
            number = code[d, s] >> 6
            if s < fcap:
                fwd = faces[want].reshape(64, c)
                back = grad_faces[jnp.where(number > 0, number - 1, no_face)].reshape(64, c)
            else:
                fwd = lines[want]
                back = grad_lines[jnp.where(number > 0, number - 1 - no_face, no_line)]
            rows.append(jnp.concatenate([fwd, back], axis=1))
        out[d] = jnp.concatenate(rows, axis=0).astype(BF16)
        return carry

    lax.fori_loop(0, owners, one, 0)


def lay_forward(weight, flat):
    c = weight.shape[1]
    for kxy in range(9):
        for kz in range(3):
            lane = (kxy * 4 + kz) * c
            flat[:, lane : lane + c] = weight[kxy * 3 + kz]
        flat[:, (kxy * 4 + 3) * c : (kxy * 4 + 4) * c] = jnp.zeros((c, c), BF16)


def lay_back(weight, flat):
    c = weight.shape[1]
    for kx in range(3):
        for ky in range(3):
            row = (kx * 4 + ky) * c
            for kz in range(3):
                flat[row : row + c, kz * c : (kz + 1) * c] = weight[kx * 9 + ky * 3 + kz]
        flat[(kx * 4 + 3) * c : (kx * 4 + 4) * c, :] = jnp.zeros((c, 3 * c), BF16)


def unpack(arrived, got_faces, got_lines, fcap, lcap):
    owners = arrived.shape[0]

    def one(d, carry):
        block = arrived[d].astype(F32)
        for s in range(fcap):
            got_faces[d * fcap + s] = block[s * 64 : (s + 1) * 64].reshape(8, 8, -1)
        base = fcap * 64
        for s in range(lcap):
            got_lines[d * lcap + s] = block[base + s * 8 : base + (s + 1) * 8]
        return carry

    lax.fori_loop(0, owners, one, 0)


def build_columns(cube, tile, pos, caps, got_faces, got_lines, block, wide, cols):
    c = cube.shape[-1]
    fcap, lcap, face_count = caps
    block[1:9, 1:9, 8:16, :] = cube
    for f in range(6):
        at = pos[tile * 6 + f]
        piece = got_faces[(at >> 8) * fcap + (at & 255)][:, :, :c]
        end = 9 * (f % 2)
        if f // 2 == 0:
            block[end, 1:9, 8:16, :] = piece
        elif f // 2 == 1:
            block[1:9, end, 8:16, :] = piece
        else:
            block[1:9, 1:9, 7 + end, :] = piece
    for e, vector in enumerate(EXTRA):
        at = pos[face_count + tile * 20 + e]
        piece = got_lines[(at >> 8) * lcap + (at & 255)][:, :c]
        px, py, pz = [9 if d > 0 else 0 for d in vector]
        if vector[2] == 0:
            block[px, py, 8:16, :] = piece
        elif vector[1] == 0:
            block[px, 1:9, 7 + pz, :] = piece
        elif vector[0] == 0:
            block[1:9, py, 7 + pz, :] = piece
        else:
            spot = 0 if vector[2] > 0 else 7
            block[px, py, 7 + pz : 8 + pz, :] = piece[spot : spot + 1]
    for kz in range(3):
        wide[:, :, :, kz * c : (kz + 1) * c] = block[:, :, 7 + kz : 15 + kz, :]
    for kxy in range(9):
        kx, ky = kxy // 3, kxy % 3
        window = wide[kx : kx + 8, ky : ky + 8].reshape(512, 4 * c).astype(BF16)
        cols[tile * 512 : (tile + 1) * 512, kxy * 4 * c : (kxy + 1) * 4 * c] = window


def fold_pieces(asked, fcap, got_faces, got_lines, face_sums, line_sums, own, tiles):
    owners = asked.shape[0]
    lcap = asked.shape[1] - fcap
    c = own.shape[-1]
    face_sums[...] = jnp.zeros_like(face_sums)
    line_sums[...] = jnp.zeros_like(line_sums)

    def one(d, carry):
        for s in range(fcap):
            to = asked[d, s] & 63
            face_sums[to] = face_sums[to] + got_faces[d * fcap + s]
        for s in range(lcap):
            to = asked[d, fcap + s] & 63
            line_sums[to] = line_sums[to] + got_lines[d * lcap + s]
        return carry

    lax.fori_loop(0, owners, one, 0)
    for tile in range(tiles):
        for f in range(6):
            piece = face_sums[tile * 6 + f][:, :, c:]
            end = 7 * (f % 2)
            if f // 2 == 0:
                own[tile, end] += piece
            elif f // 2 == 1:
                own[tile, :, end] += piece
            else:
                own[tile, :, :, end, :] += piece
        for main in range(3):
            for b1 in range(2):
                for b2 in range(2):
                    piece = line_sums[tile * 12 + main * 4 + b1 * 2 + b2][:, c:]
                    if main == 2:
                        own[tile, 7 * b1, 7 * b2] += piece
                    elif main == 1:
                        own[tile, 7 * b1, :, 7 * b2, :] += piece
                    else:
                        own[tile, :, 7 * b1, 7 * b2, :] += piece


def deal_term(upstream, cols, terms):
    c = upstream.shape[0]
    term = jnp.dot(upstream, cols[...], preferred_element_type=F32)
    owners = terms.shape[0]
    share = terms.shape[2] // c
    for d in range(owners):
        parts = []
        for k in DEAL[d * share : (d + 1) * share]:
            lane = (k // 3) * 4 * c + (k % 3) * c
            parts.append(term[:, lane : lane + c])
        while len(parts) < share:
            parts.append(jnp.zeros((c, c), F32))
        terms[d] = (parts[0] if share == 1 else jnp.concatenate(parts, axis=1))


def first_kernel(fcap, asked, code, feat, occ, cot, weight, out, rows, own,
                 faces, lines, grad_faces, grad_lines, wide, spread, wb):
    tiles, c = feat.shape[0], feat.shape[1]
    lay_back(weight, wb)
    wide[...] = jnp.zeros_like(wide)
    grad_faces[tiles * 6] = jnp.zeros((8, 8, c), F32)
    grad_lines[tiles * 20] = jnp.zeros((8, c), F32)
    for t in range(tiles):
        live = occ[t : t + 1, :].astype(F32)
        masked = (feat[t].astype(F32) * live).T
        rows[t] = masked.reshape(64, 8, c)
        cut_pieces(masked.reshape(8, 8, 8, c), t, faces, lines)
        upstream = (cot[t].astype(F32) * live).T
        conv_back(upstream, wb, wide, spread, t, own, grad_faces, grad_lines)
    fill_outgoing(asked, code, fcap, out, faces, lines, grad_faces, grad_lines)


def second_kernel(fcap, asked, code, pos, arrived, rows, own_in, occ, weight,
                  out, hidden_rows, own_out, terms,
                  faces, lines, grad_faces, grad_lines, wide_back, spread, wb,
                  got_faces, got_lines, face_sums, line_sums, block, wide, cols, own, wf):
    tiles, c = rows.shape[0], rows.shape[3]
    lcap = asked.shape[1] - fcap
    caps = (fcap, lcap, tiles * 6)
    lay_back(weight, wb)
    lay_forward(weight, wf)
    wide_back[...] = jnp.zeros_like(wide_back)
    wide[:, :, :, 3 * c :] = jnp.zeros((10, 10, 8, c), F32)
    grad_faces[tiles * 6] = jnp.zeros((8, 8, c), F32)
    grad_lines[tiles * 20] = jnp.zeros((8, c), F32)
    unpack(arrived, got_faces, got_lines, fcap, lcap)
    for t in range(tiles):
        own[t] = own_in[t].reshape(8, 8, 8, c)
        build_columns(rows[t].reshape(8, 8, 8, c), t, pos, caps, got_faces, got_lines, block, wide, cols)
    fold_pieces(asked, fcap, got_faces, got_lines, face_sums, line_sums, own, tiles)
    conv = lax.dot_general(wf[...], cols[...], (((1,), (1,)), ((), ())), preferred_element_type=F32)
    grads = []
    for t in range(tiles):
        live = occ[t : t + 1, :].astype(F32)
        pre = live * conv[:, t * 512 : (t + 1) * 512]
        logistic = 1.0 / (1.0 + jnp.exp(-pre))
        hidden = (pre * logistic).astype(BF16).astype(F32).T
        hidden_rows[t] = hidden.reshape(64, 8, c)
        cut_pieces(hidden.reshape(8, 8, 8, c), t, faces, lines)
        grad = own[t].reshape(512, c).T
        act = (grad * live * logistic * (1.0 + pre * (1.0 - logistic))).astype(BF16)
        grads.append(act)
        conv_back(act.astype(F32).T, wb, wide_back, spread, t, own_out, grad_faces, grad_lines)
    fill_outgoing(asked, code, fcap, out, faces, lines, grad_faces, grad_lines)
    deal_term(jnp.concatenate(grads, axis=1), cols, terms)


def third_kernel(fcap, asked, pos, arrived, hidden_rows, own_in, occ, feat, cot, weight,
                 block_out, feature_grad, terms,
                 got_faces, got_lines, face_sums, line_sums, block, wide, cols, own, wf):
    tiles, c = feat.shape[0], feat.shape[1]
    lcap = asked.shape[1] - fcap
    caps = (fcap, lcap, tiles * 6)
    lay_forward(weight, wf)
    wide[:, :, :, 3 * c :] = jnp.zeros((10, 10, 8, c), F32)
    unpack(arrived, got_faces, got_lines, fcap, lcap)
    grads = []
    for t in range(tiles):
        own[t] = own_in[t].reshape(8, 8, 8, c)
        build_columns(hidden_rows[t].reshape(8, 8, 8, c), t, pos, caps, got_faces, got_lines, block, wide, cols)
        grads.append((cot[t].astype(F32) * occ[t : t + 1, :].astype(F32)).astype(BF16))
    deal_term(jnp.concatenate(grads, axis=1), cols, terms)
    conv = lax.dot_general(wf[...], cols[...], (((1,), (1,)), ((), ())), preferred_element_type=F32)
    fold_pieces(asked, fcap, got_faces, got_lines, face_sums, line_sums, own, tiles)
    for t in range(tiles):
        live = occ[t : t + 1, :].astype(F32)
        branch = live * conv[:, t * 512 : (t + 1) * 512]
        block_out[t] = (feat[t].astype(F32) * live + branch).astype(BF16)
        sums = own[t].reshape(512, c).T
        feature_grad[t] = ((cot[t].astype(F32) + sums) * live).astype(BF16)


def remote(src, dst, send, recv, device):
    return pltpu.make_async_remote_copy(
        src_ref=src, dst_ref=dst, send_sem=send, recv_sem=recv,
        device_id=device, device_id_type=pl.DeviceIdType.MESH)


def exchange_kernel(outgoing, arrived, send, recv, local):
    owners = outgoing.shape[0]
    subs = lax.axis_size("sub")
    me = lax.axis_index("space") * subs + lax.axis_index("sub")

    def place(i):
        peer = lax.rem(me + i, owners)
        return peer, {"space": peer // subs, "sub": lax.rem(peer, subs)}

    barrier = pltpu.get_barrier_semaphore()
    for i in range(1, owners):
        pl.semaphore_signal(barrier, inc=1, device_id=place(i)[1], device_id_type=pl.DeviceIdType.MESH)
    own = pltpu.make_async_copy(outgoing.at[me], arrived.at[me], local)
    own.start()
    pl.semaphore_wait(barrier, owners - 1)
    order = sorted(range(1, owners), key=lambda i: abs(i - owners // 2))
    copies = []
    for i in order:
        peer, device = place(i)
        copy = remote(outgoing.at[peer], arrived.at[me], send.at[i], recv.at[i], device)
        copy.start()
        copies.append(copy)
    own.wait()
    for copy in copies:
        copy.wait()


def exchange(outgoing, number):
    owners = outgoing.shape[0]
    place = pl.BlockSpec(memory_space=pl.ANY)
    return pl.pallas_call(
        exchange_kernel,
        out_shape=jax.ShapeDtypeStruct(outgoing.shape, outgoing.dtype),
        in_specs=[place],
        out_specs=place,
        scratch_shapes=[
            pltpu.SemaphoreType.DMA((owners,)),
            pltpu.SemaphoreType.DMA((owners,)),
            pltpu.SemaphoreType.DMA,
        ],
        compiler_params=pltpu.CompilerParams(collective_id=number, has_side_effects=True),
    )(outgoing)


def reduce_kernel(scale, first, second, first_out, second_out, halves, sums, parts, gathered,
                  half_send, half_recv, part_send, part_recv, gather_send, gather_recv,
                  last_send, last_recv):
    spaces, c = sums.shape[0], sums.shape[2]
    space, sub = lax.axis_index("space"), lax.axis_index("sub")
    other = 1 - sub
    partner = {"space": space, "sub": other}

    def peer(i):
        at = lax.rem(space + i, spaces)
        return at, {"space": at, "sub": sub}

    barrier = pltpu.get_barrier_semaphore()
    pl.semaphore_signal(barrier, inc=1, device_id=partner, device_id_type=pl.DeviceIdType.MESH)
    for i in range(1, spaces):
        pl.semaphore_signal(barrier, inc=1, device_id=peer(i)[1], device_id_type=pl.DeviceIdType.MESH)
    pl.semaphore_wait(barrier, spaces)
    copies = []
    for j, term in enumerate((first, second)):
        copy = remote(term.at[pl.ds(other * spaces, spaces)], halves.at[j],
                      half_send.at[j], half_recv.at[j], partner)
        copy.start()
        copies.append(copy)
    for copy in copies:
        copy.wait()
    for j, term in enumerate((first, second)):
        for s in range(spaces):
            sums[s, j] = (term[sub * spaces + s] + halves[j, s]).astype(BF16)
    order = sorted(range(1, spaces), key=lambda i: abs(i - spaces // 2))
    copies = []
    for i in order:
        at, device = peer(i)
        copy = remote(sums.at[at], parts.at[space], part_send.at[i], part_recv.at[i], device)
        copy.start()
        copies.append(copy)
    parts[space] = sums[space]
    for copy in copies:
        copy.wait()
    total = parts[0].astype(F32)
    for s in range(1, spaces):
        total = total + parts[s].astype(F32)
    gathered[sub, space] = (total * scale).astype(BF16)
    copies = []
    for i in order:
        at, device = peer(i)
        copy = remote(gathered.at[sub, space], gathered.at[sub, space],
                      gather_send.at[i], gather_recv.at[i], device)
        copy.start()
        copies.append(copy)
    lasts = []

    def hand_on(i):
        at = lax.rem(space - i + spaces, spaces)
        copy = remote(gathered.at[sub, at], gathered.at[sub, at], last_send.at[i], last_recv.at[i], partner)
        copy.start()
        lasts.append(copy)

    hand_on(0)
    for i, copy in reversed(list(zip(order, copies))):
        copy.wait_recv()
        hand_on(i)
    for copy in copies:
        copy.wait_send()
    for copy in lasts:
        copy.wait()
    share = gathered.shape[4] // c
    for at, k in enumerate(DEAL):
        owner, lane = at // share, at % share * c
        for j, out in enumerate((first_out, second_out)):
            out[k] = gathered[owner // spaces, owner % spaces, j][:, lane : lane + c].astype(F32)


def reduce_terms(first, second, scale, number):
    subs, spaces = lax.axis_size("sub"), lax.axis_size("space")
    owners, c, width = first.shape
    vmem = pl.BlockSpec(memory_space=pltpu.VMEM)
    dma = pltpu.SemaphoreType.DMA
    return pl.pallas_call(
        lambda *refs: reduce_kernel(scale, *refs),
        out_shape=(jax.ShapeDtypeStruct((27, c, c), F32),) * 2,
        in_specs=[vmem] * 2,
        out_specs=(vmem,) * 2,
        scratch_shapes=[
            pltpu.VMEM((2, spaces, c, width), F32),
            pltpu.VMEM((spaces, 2, c, width), BF16),
            pltpu.VMEM((spaces, 2, c, width), BF16),
            pltpu.VMEM((subs, spaces, 2, c, width), BF16),
            dma((2,)), dma((2,)), dma((spaces,)), dma((spaces,)),
            dma((spaces,)), dma((spaces,)), dma((spaces,)), dma((spaces,)),
        ],
        compiler_params=pltpu.CompilerParams(
            collective_id=number, has_side_effects=True, vmem_limit_bytes=32 * 1024 * 1024),
    )(first, second)


def plan(owner, want, owners, faces, fcap, lcap):
    count = owner.shape[0]
    cap = fcap + lcap
    at = jnp.arange(count, dtype=jnp.int32)
    line = (at >= faces).astype(jnp.int32)
    group = owner * 2 + line
    earlier = (at[None, :] < at[:, None]) & (group[None, :] == group[:, None])
    rank = jnp.sum(earlier.astype(jnp.int32), axis=1)
    slot = owner * cap + line * fcap + rank
    hit = slot[None, :] == jnp.arange(owners * cap, dtype=jnp.int32)[:, None]
    code = jnp.sum(jnp.where(hit, (at * 64 + 64 + want)[None, :], 0), axis=1)
    return owner * 256 + rank, code.reshape(owners, cap)


def body(features, occupancy, face_owner, face_slot, line_owner, line_slot, weight_one, weight_two, cotangent):
    owners = lax.axis_size(OWNER_AXES)
    tiles, c = features.shape[0], features.shape[1]
    fcap = max(2, 30 * tiles // (4 * owners) + 1)
    lcap = max(2, 100 * tiles // (4 * owners) + 1)
    share = -(-27 // owners)
    height = fcap * 64 + lcap * 8
    opposite = jnp.array(OPPOSITE, jnp.int32)
    need = jnp.array(line_need(), jnp.int32)
    owner = jnp.concatenate([face_owner.reshape(-1), line_owner.reshape(-1)])
    want = jnp.concatenate([
        (face_slot * 6 + opposite[None, :]).reshape(-1), (line_slot * 12 + need[None, :]).reshape(-1)])
    pos, code = plan(owner, want, owners, tiles * 6, fcap, lcap)
    sent = jnp.broadcast_to(jnp.pad(code, ((0, 0), (0, 128 - fcap - lcap)))[:, None, :], (owners, 8, 128))
    asked = exchange(sent, 3)[:, 0, : fcap + lcap]

    smem = pl.BlockSpec(memory_space=pltpu.SMEM)
    vmem = pl.BlockSpec(memory_space=pltpu.VMEM)
    params = pltpu.CompilerParams(vmem_limit_bytes=56 * 1024 * 1024)
    shape = jax.ShapeDtypeStruct
    table_scratch = [
        pltpu.VMEM((tiles * 6, 8, 8, c), F32),
        pltpu.VMEM((tiles * 12, 8, c), F32),
        pltpu.VMEM((tiles * 6 + 1, 8, 8, c), F32),
        pltpu.VMEM((tiles * 20 + 1, 8, c), F32),
        pltpu.VMEM((12, 10, 8, 4 * c), F32),
        pltpu.VMEM((10, 10, 24, c), F32),
        pltpu.VMEM((12 * c, 3 * c), BF16),
    ]
    got_scratch = [
        pltpu.VMEM((owners * fcap, 8, 8, 2 * c), F32),
        pltpu.VMEM((owners * lcap, 8, 2 * c), F32),
        pltpu.VMEM((tiles * 6, 8, 8, 2 * c), F32),
        pltpu.VMEM((tiles * 12, 8, 2 * c), F32),
        pltpu.VMEM((10, 10, 24, c), F32),
        pltpu.VMEM((10, 10, 8, 4 * c), F32),
        pltpu.VMEM((tiles * 512, 36 * c), BF16),
        pltpu.VMEM((tiles, 8, 8, 8, c), F32),
        pltpu.VMEM((c, 36 * c), BF16),
    ]
    out_block = shape((owners, height, 2 * c), BF16)
    row_block = shape((tiles, 64, 8, c), F32)
    term_block = shape((owners, c, share * c), F32)
    volume = shape(features.shape, BF16)

    outgoing, rows, hidden_own = pl.pallas_call(
        lambda *refs: first_kernel(fcap, *refs),
        out_shape=(out_block, row_block, row_block),
        in_specs=[smem] * 2 + [vmem] * 4,
        out_specs=(vmem,) * 3,
        scratch_shapes=table_scratch,
        compiler_params=params,
    )(asked, code, features, occupancy, cotangent, weight_two)
    arrived = exchange(outgoing, 0)
    outgoing, hidden_rows, feature_own, first_term = pl.pallas_call(
        lambda *refs: second_kernel(fcap, *refs),
        out_shape=(out_block, row_block, row_block, term_block),
        in_specs=[smem] * 3 + [vmem] * 5,
        out_specs=(vmem,) * 4,
        scratch_shapes=table_scratch + got_scratch,
        compiler_params=params,
    )(asked, code, pos, arrived, rows, hidden_own, occupancy, weight_one)
    arrived = exchange(outgoing, 1)
    block_out, feature_grad, second_term = pl.pallas_call(
        lambda *refs: third_kernel(fcap, *refs),
        out_shape=(volume, volume, term_block),
        in_specs=[smem] * 2 + [vmem] * 7,
        out_specs=(vmem,) * 3,
        scratch_shapes=got_scratch,
        compiler_params=params,
    )(asked, pos, arrived, hidden_rows, feature_own, occupancy, features, cotangent, weight_two)
    grad_scale = 1.0 / math.sqrt(512.0 * tiles * owners)
    first_grad, second_grad = reduce_terms(first_term, second_term, grad_scale, 2)
    return (block_out, feature_grad, first_grad, second_grad)


def solution(mesh):
    split = P(("scene", "space", "sub"), None, None)
    split2 = P(("scene", "space", "sub"), None)
    in_specs = (split, split2, split, split2, split, split2, P(), P(), split)
    out_specs = (split, split, P("scene", None, None), P("scene", None, None))
    return jax.shard_map(body, mesh=mesh, in_specs=in_specs, out_specs=out_specs, check_vma=False)
```

```python
import math

import jax
import jax.numpy as jnp
from jax import lax
from jax.experimental import pallas as pl
from jax.experimental.pallas import tpu as pltpu
from jax.sharding import PartitionSpec as P

F32 = jnp.float32
BF16 = jnp.bfloat16
OWNER_AXES = ("space", "sub")

_VECTORS = [(x, y, z) for x in (-1, 0, 1) for y in (-1, 0, 1) for z in (-1, 0, 1)]
EXTRA = [v for v in _VECTORS if sum(c != 0 for c in v) == 2]
EXTRA = EXTRA + [v for v in _VECTORS if sum(c != 0 for c in v) == 3]
OPPOSITE = (1, 0, 3, 2, 5, 4)


def line_need():
    need = []
    for vector in EXTRA:
        zero = [a for a in range(3) if vector[a] == 0]
        main = zero[0] if zero else 2
        rest = [a for a in range(3) if a != main]
        b1 = 0 if vector[rest[0]] > 0 else 1
        b2 = 0 if vector[rest[1]] > 0 else 1
        need.append(main * 4 + b1 * 2 + b2)
    return need


DEAL = [k for k in range(27) if k % 3 < 2] + [k for k in range(27) if k % 3 == 2]


def cut_pieces(values, tile, faces, lines):
    for f in range(6):
        end = 7 * (f % 2)
        if f // 2 == 0:
            piece = values[end]
        elif f // 2 == 1:
            piece = values[:, end]
        else:
            piece = values[:, :, end, :]
        faces[tile * 6 + f] = piece
    for main in range(3):
        for b1 in range(2):
            for b2 in range(2):
                if main == 2:
                    piece = values[7 * b1, 7 * b2]
                elif main == 1:
                    piece = values[7 * b1, :, 7 * b2, :]
                else:
                    piece = values[:, 7 * b1, 7 * b2, :]
                lines[tile * 12 + main * 4 + b1 * 2 + b2] = piece


def conv_back(up_rows, weight, wide, spread, tile, own, grad_faces, grad_lines):
    c = up_rows.shape[-1]
    cube = up_rows.reshape(8, 8, 8, c)
    for j in range(3):
        wide[2:10, j : j + 8, :, j * c : (j + 1) * c] = cube
    total = None
    for kx in range(3):
        cols = wide[2 - kx : 12 - kx].reshape(800, 4 * c).astype(BF16)
        term = jnp.dot(cols, weight[kx * 4 * c : (kx + 1) * 4 * c, :], preferred_element_type=F32)
        total = term if total is None else total + term
    total = total.reshape(10, 10, 8, 3 * c)
    spread[:, :, 16:24, :] = jnp.zeros((10, 10, 8, c), F32)
    spread[:, :, 8:16, :] = total[:, :, :, :c]
    spread[:, :, 9:17, :] += total[:, :, :, c : 2 * c]
    spread[:, :, 10:18, :] += total[:, :, :, 2 * c :]
    own[tile] = spread[1:9, 1:9, 9:17, :].reshape(64, 8, c)
    for f in range(6):
        end = 9 * (f % 2)
        if f // 2 == 0:
            piece = spread[end, 1:9, 9:17, :]
        elif f // 2 == 1:
            piece = spread[1:9, end, 9:17, :]
        else:
            piece = spread[1:9, 1:9, 8 + end, :]
        grad_faces[tile * 6 + f] = piece
    for e, vector in enumerate(EXTRA):
        px, py, pz = [9 if d > 0 else 0 for d in vector]
        if vector[2] == 0:
            piece = spread[px, py, 9:17, :]
        elif vector[1] == 0:
            piece = spread[px, 1:9, 8 + pz, :]
        elif vector[0] == 0:
            piece = spread[1:9, py, 8 + pz, :]
        else:
            row = spread[px, py, 8 + pz : 9 + pz, :]
            spot = 0 if vector[2] > 0 else 7
            at = lax.broadcasted_iota(jnp.int32, (8, c), 0)
            piece = jnp.where(at == spot, jnp.broadcast_to(row, (8, c)), 0.0)
        grad_lines[tile * 20 + e] = piece


def fill_outgoing(asked, code, fcap, out, faces, lines, grad_faces, grad_lines):
    owners, cap = asked.shape
    c = faces.shape[-1]
    no_face, no_line = grad_faces.shape[0] - 1, grad_lines.shape[0] - 1

    def one(d, carry):
        rows = []
        for s in range(cap):
            want = asked[d, s] & 63
            number = code[d, s] >> 6
            if s < fcap:
                fwd = faces[want].reshape(64, c)
                back = grad_faces[jnp.where(number > 0, number - 1, no_face)].reshape(64, c)
            else:
                fwd = lines[want]
                back = grad_lines[jnp.where(number > 0, number - 1 - no_face, no_line)]
            rows.append(jnp.concatenate([fwd, back], axis=1))
        out[d] = jnp.concatenate(rows, axis=0).astype(BF16)
        return carry

    lax.fori_loop(0, owners, one, 0)


def lay_forward(weight, flat):
    c = weight.shape[1]
    for kxy in range(9):
        for kz in range(3):
            lane = (kxy * 4 + kz) * c
            flat[:, lane : lane + c] = weight[kxy * 3 + kz]
        flat[:, (kxy * 4 + 3) * c : (kxy * 4 + 4) * c] = jnp.zeros((c, c), BF16)


def lay_back(weight, flat):
    c = weight.shape[1]
    for kx in range(3):
        for ky in range(3):
            row = (kx * 4 + ky) * c
            for kz in range(3):
                flat[row : row + c, kz * c : (kz + 1) * c] = weight[kx * 9 + ky * 3 + kz]
        flat[(kx * 4 + 3) * c : (kx * 4 + 4) * c, :] = jnp.zeros((c, 3 * c), BF16)


def unpack(arrived, got_faces, got_lines, fcap, lcap):
    owners = arrived.shape[0]

    def one(d, carry):
        block = arrived[d].astype(F32)
        for s in range(fcap):
            got_faces[d * fcap + s] = block[s * 64 : (s + 1) * 64].reshape(8, 8, -1)
        base = fcap * 64
        for s in range(lcap):
            got_lines[d * lcap + s] = block[base + s * 8 : base + (s + 1) * 8]
        return carry

    lax.fori_loop(0, owners, one, 0)


def build_columns(cube, tile, pos, caps, got_faces, got_lines, block, wide, cols):
    c = cube.shape[-1]
    fcap, lcap, face_count = caps
    block[1:9, 1:9, 8:16, :] = cube
    for f in range(6):
        at = pos[tile * 6 + f]
        piece = got_faces[(at >> 8) * fcap + (at & 255)][:, :, :c]
        end = 9 * (f % 2)
        if f // 2 == 0:
            block[end, 1:9, 8:16, :] = piece
        elif f // 2 == 1:
            block[1:9, end, 8:16, :] = piece
        else:
            block[1:9, 1:9, 7 + end, :] = piece
    for e, vector in enumerate(EXTRA):
        at = pos[face_count + tile * 20 + e]
        piece = got_lines[(at >> 8) * lcap + (at & 255)][:, :c]
        px, py, pz = [9 if d > 0 else 0 for d in vector]
        if vector[2] == 0:
            block[px, py, 8:16, :] = piece
        elif vector[1] == 0:
            block[px, 1:9, 7 + pz, :] = piece
        elif vector[0] == 0:
            block[1:9, py, 7 + pz, :] = piece
        else:
            spot = 0 if vector[2] > 0 else 7
            block[px, py, 7 + pz : 8 + pz, :] = piece[spot : spot + 1]
    for kz in range(3):
        wide[:, :, :, kz * c : (kz + 1) * c] = block[:, :, 7 + kz : 15 + kz, :]
    for kxy in range(9):
        kx, ky = kxy // 3, kxy % 3
        window = wide[kx : kx + 8, ky : ky + 8].reshape(512, 4 * c).astype(BF16)
        cols[tile * 512 : (tile + 1) * 512, kxy * 4 * c : (kxy + 1) * 4 * c] = window


def fold_pieces(asked, fcap, got_faces, got_lines, face_sums, line_sums, own, tiles):
    owners = asked.shape[0]
    lcap = asked.shape[1] - fcap
    c = own.shape[-1]
    face_sums[...] = jnp.zeros_like(face_sums)
    line_sums[...] = jnp.zeros_like(line_sums)

    def one(d, carry):
        for s in range(fcap):
            to = asked[d, s] & 63
            face_sums[to] = face_sums[to] + got_faces[d * fcap + s]
        for s in range(lcap):
            to = asked[d, fcap + s] & 63
            line_sums[to] = line_sums[to] + got_lines[d * lcap + s]
        return carry

    lax.fori_loop(0, owners, one, 0)
    for tile in range(tiles):
        for f in range(6):
            piece = face_sums[tile * 6 + f][:, :, c:]
            end = 7 * (f % 2)
            if f // 2 == 0:
                own[tile, end] += piece
            elif f // 2 == 1:
                own[tile, :, end] += piece
            else:
                own[tile, :, :, end, :] += piece
        for main in range(3):
            for b1 in range(2):
                for b2 in range(2):
                    piece = line_sums[tile * 12 + main * 4 + b1 * 2 + b2][:, c:]
                    if main == 2:
                        own[tile, 7 * b1, 7 * b2] += piece
                    elif main == 1:
                        own[tile, 7 * b1, :, 7 * b2, :] += piece
                    else:
                        own[tile, :, 7 * b1, 7 * b2, :] += piece


def deal_term(upstream, cols, terms):
    c = upstream.shape[0]
    term = jnp.dot(upstream, cols[...], preferred_element_type=F32)
    owners = terms.shape[0]
    share = terms.shape[2] // c
    for d in range(owners):
        parts = []
        for k in DEAL[d * share : (d + 1) * share]:
            lane = (k // 3) * 4 * c + (k % 3) * c
            parts.append(term[:, lane : lane + c])
        while len(parts) < share:
            parts.append(jnp.zeros((c, c), F32))
        terms[d] = (parts[0] if share == 1 else jnp.concatenate(parts, axis=1))


def first_kernel(fcap, asked, code, feat, occ, cot, weight, out, rows, own,
                 faces, lines, grad_faces, grad_lines, wide, spread, wb):
    tiles, c = feat.shape[0], feat.shape[1]
    lay_back(weight, wb)
    wide[...] = jnp.zeros_like(wide)
    grad_faces[tiles * 6] = jnp.zeros((8, 8, c), F32)
    grad_lines[tiles * 20] = jnp.zeros((8, c), F32)
    for t in range(tiles):
        live = occ[t : t + 1, :].astype(F32)
        masked = (feat[t].astype(F32) * live).T
        rows[t] = masked.reshape(64, 8, c)
        cut_pieces(masked.reshape(8, 8, 8, c), t, faces, lines)
        upstream = (cot[t].astype(F32) * live).T
        conv_back(upstream, wb, wide, spread, t, own, grad_faces, grad_lines)
    fill_outgoing(asked, code, fcap, out, faces, lines, grad_faces, grad_lines)


def second_kernel(fcap, asked, code, pos, arrived, rows, own_in, occ, weight,
                  out, hidden_rows, own_out, terms,
                  faces, lines, grad_faces, grad_lines, wide_back, spread, wb,
                  got_faces, got_lines, face_sums, line_sums, block, wide, cols, own, wf):
    tiles, c = rows.shape[0], rows.shape[3]
    lcap = asked.shape[1] - fcap
    caps = (fcap, lcap, tiles * 6)
    lay_back(weight, wb)
    lay_forward(weight, wf)
    wide_back[...] = jnp.zeros_like(wide_back)
    wide[:, :, :, 3 * c :] = jnp.zeros((10, 10, 8, c), F32)
    grad_faces[tiles * 6] = jnp.zeros((8, 8, c), F32)
    grad_lines[tiles * 20] = jnp.zeros((8, c), F32)
    unpack(arrived, got_faces, got_lines, fcap, lcap)
    for t in range(tiles):
        own[t] = own_in[t].reshape(8, 8, 8, c)
        build_columns(rows[t].reshape(8, 8, 8, c), t, pos, caps, got_faces, got_lines, block, wide, cols)
    fold_pieces(asked, fcap, got_faces, got_lines, face_sums, line_sums, own, tiles)
    conv = lax.dot_general(wf[...], cols[...], (((1,), (1,)), ((), ())), preferred_element_type=F32)
    grads = []
    for t in range(tiles):
        live = occ[t : t + 1, :].astype(F32)
        pre = live * conv[:, t * 512 : (t + 1) * 512]
        logistic = 1.0 / (1.0 + jnp.exp(-pre))
        hidden = (pre * logistic).astype(BF16).astype(F32).T
        hidden_rows[t] = hidden.reshape(64, 8, c)
        cut_pieces(hidden.reshape(8, 8, 8, c), t, faces, lines)
        grad = own[t].reshape(512, c).T
        act = (grad * live * logistic * (1.0 + pre * (1.0 - logistic))).astype(BF16)
        grads.append(act)
        conv_back(act.astype(F32).T, wb, wide_back, spread, t, own_out, grad_faces, grad_lines)
    fill_outgoing(asked, code, fcap, out, faces, lines, grad_faces, grad_lines)
    deal_term(jnp.concatenate(grads, axis=1), cols, terms)


def third_kernel(fcap, asked, pos, arrived, hidden_rows, own_in, occ, feat, cot, weight,
                 block_out, feature_grad, terms,
                 got_faces, got_lines, face_sums, line_sums, block, wide, cols, own, wf):
    tiles, c = feat.shape[0], feat.shape[1]
    lcap = asked.shape[1] - fcap
    caps = (fcap, lcap, tiles * 6)
    lay_forward(weight, wf)
    wide[:, :, :, 3 * c :] = jnp.zeros((10, 10, 8, c), F32)
    unpack(arrived, got_faces, got_lines, fcap, lcap)
    grads = []
    for t in range(tiles):
        own[t] = own_in[t].reshape(8, 8, 8, c)
        build_columns(hidden_rows[t].reshape(8, 8, 8, c), t, pos, caps, got_faces, got_lines, block, wide, cols)
        grads.append((cot[t].astype(F32) * occ[t : t + 1, :].astype(F32)).astype(BF16))
    deal_term(jnp.concatenate(grads, axis=1), cols, terms)
    conv = lax.dot_general(wf[...], cols[...], (((1,), (1,)), ((), ())), preferred_element_type=F32)
    fold_pieces(asked, fcap, got_faces, got_lines, face_sums, line_sums, own, tiles)
    for t in range(tiles):
        live = occ[t : t + 1, :].astype(F32)
        branch = live * conv[:, t * 512 : (t + 1) * 512]
        block_out[t] = (feat[t].astype(F32) * live + branch).astype(BF16)
        sums = own[t].reshape(512, c).T
        feature_grad[t] = ((cot[t].astype(F32) + sums) * live).astype(BF16)


def remote(src, dst, send, recv, device):
    return pltpu.make_async_remote_copy(
        src_ref=src, dst_ref=dst, send_sem=send, recv_sem=recv,
        device_id=device, device_id_type=pl.DeviceIdType.MESH)


def exchange_kernel(outgoing, arrived, send, recv, local):
    owners = outgoing.shape[0]
    subs = lax.axis_size("sub")
    me = lax.axis_index("space") * subs + lax.axis_index("sub")

    def place(i):
        peer = lax.rem(me + i, owners)
        return peer, {"space": peer // subs, "sub": lax.rem(peer, subs)}

    barrier = pltpu.get_barrier_semaphore()
    for i in range(1, owners):
        pl.semaphore_signal(barrier, inc=1, device_id=place(i)[1], device_id_type=pl.DeviceIdType.MESH)
    own = pltpu.make_async_copy(outgoing.at[me], arrived.at[me], local)
    own.start()
    pl.semaphore_wait(barrier, owners - 1)
    order = sorted(range(1, owners), key=lambda i: abs(i - owners // 2))
    copies = []
    for i in order:
        peer, device = place(i)
        copy = remote(outgoing.at[peer], arrived.at[me], send.at[i], recv.at[i], device)
        copy.start()
        copies.append(copy)
    own.wait()
    for copy in copies:
        copy.wait()


def exchange(outgoing, number):
    owners = outgoing.shape[0]
    place = pl.BlockSpec(memory_space=pl.ANY)
    return pl.pallas_call(
        exchange_kernel,
        out_shape=jax.ShapeDtypeStruct(outgoing.shape, outgoing.dtype),
        in_specs=[place],
        out_specs=place,
        scratch_shapes=[
            pltpu.SemaphoreType.DMA((owners,)),
            pltpu.SemaphoreType.DMA((owners,)),
            pltpu.SemaphoreType.DMA,
        ],
        compiler_params=pltpu.CompilerParams(collective_id=number, has_side_effects=True),
    )(outgoing)


def reduce_kernel(scale, first, second, first_out, second_out, halves, sums, parts, gathered,
                  half_send, half_recv, part_send, part_recv, gather_send, gather_recv,
                  last_send, last_recv):
    spaces, c = sums.shape[0], sums.shape[2]
    space, sub = lax.axis_index("space"), lax.axis_index("sub")
    other = 1 - sub
    partner = {"space": space, "sub": other}

    def peer(i):
        at = lax.rem(space + i, spaces)
        return at, {"space": at, "sub": sub}

    barrier = pltpu.get_barrier_semaphore()
    pl.semaphore_signal(barrier, inc=1, device_id=partner, device_id_type=pl.DeviceIdType.MESH)
    for i in range(1, spaces):
        pl.semaphore_signal(barrier, inc=1, device_id=peer(i)[1], device_id_type=pl.DeviceIdType.MESH)
    pl.semaphore_wait(barrier, spaces)
    order = sorted(range(1, spaces), key=lambda i: abs(i - spaces // 2))
    pieces = []
    for i in order + [0]:
        at = lax.rem(space + i, spaces)
        for j, term in enumerate((first, second)):
            copy = remote(term.at[other * spaces + at], halves.at[j, at],
                          half_send.at[j, i], half_recv.at[j, i], partner)
            copy.start()
            pieces.append(copy)
    copies = []
    for turn, i in enumerate(order + [0]):
        at, device = peer(i)
        for j, term in enumerate((first, second)):
            pieces[2 * turn + j].wait_recv()
            sums[at, j] = (term[sub * spaces + at] + halves[j, at]).astype(BF16)
        if i:
            copy = remote(sums.at[at], parts.at[space], part_send.at[i], part_recv.at[i], device)
            copy.start()
            copies.append(copy)
        else:
            parts[space] = sums[at]
    for copy in pieces:
        copy.wait_send()
    for copy in copies:
        copy.wait()
    total = parts[0].astype(F32)
    for s in range(1, spaces):
        total = total + parts[s].astype(F32)
    gathered[sub, space] = (total * scale).astype(BF16)
    copies = []
    for i in order:
        at, device = peer(i)
        copy = remote(gathered.at[sub, space], gathered.at[sub, space],
                      gather_send.at[i], gather_recv.at[i], device)
        copy.start()
        copies.append(copy)
    lasts = []

    def hand_on(i):
        at = lax.rem(space - i + spaces, spaces)
        copy = remote(gathered.at[sub, at], gathered.at[sub, at], last_send.at[i], last_recv.at[i], partner)
        copy.start()
        lasts.append(copy)

    hand_on(0)
    for i, copy in reversed(list(zip(order, copies))):
        copy.wait_recv()
        hand_on(i)
    for copy in copies:
        copy.wait_send()
    for copy in lasts:
        copy.wait()
    share = gathered.shape[4] // c
    for at, k in enumerate(DEAL):
        owner, lane = at // share, at % share * c
        for j, out in enumerate((first_out, second_out)):
            out[k] = gathered[owner // spaces, owner % spaces, j][:, lane : lane + c].astype(F32)


def reduce_terms(first, second, scale, number):
    subs, spaces = lax.axis_size("sub"), lax.axis_size("space")
    owners, c, width = first.shape
    vmem = pl.BlockSpec(memory_space=pltpu.VMEM)
    dma = pltpu.SemaphoreType.DMA
    return pl.pallas_call(
        lambda *refs: reduce_kernel(scale, *refs),
        out_shape=(jax.ShapeDtypeStruct((27, c, c), F32),) * 2,
        in_specs=[vmem] * 2,
        out_specs=(vmem,) * 2,
        scratch_shapes=[
            pltpu.VMEM((2, spaces, c, width), F32),
            pltpu.VMEM((spaces, 2, c, width), BF16),
            pltpu.VMEM((spaces, 2, c, width), BF16),
            pltpu.VMEM((subs, spaces, 2, c, width), BF16),
            dma((2, spaces)), dma((2, spaces)), dma((spaces,)), dma((spaces,)),
            dma((spaces,)), dma((spaces,)), dma((spaces,)), dma((spaces,)),
        ],
        compiler_params=pltpu.CompilerParams(
            collective_id=number, has_side_effects=True, vmem_limit_bytes=32 * 1024 * 1024),
    )(first, second)


def plan(owner, want, owners, faces, fcap, lcap):
    count = owner.shape[0]
    cap = fcap + lcap
    at = jnp.arange(count, dtype=jnp.int32)
    line = (at >= faces).astype(jnp.int32)
    group = owner * 2 + line
    earlier = (at[None, :] < at[:, None]) & (group[None, :] == group[:, None])
    rank = jnp.sum(earlier.astype(jnp.int32), axis=1)
    slot = owner * cap + line * fcap + rank
    hit = slot[None, :] == jnp.arange(owners * cap, dtype=jnp.int32)[:, None]
    code = jnp.sum(jnp.where(hit, (at * 64 + 64 + want)[None, :], 0), axis=1)
    return owner * 256 + rank, code.reshape(owners, cap)


def body(features, occupancy, face_owner, face_slot, line_owner, line_slot, weight_one, weight_two, cotangent):
    owners = lax.axis_size(OWNER_AXES)
    tiles, c = features.shape[0], features.shape[1]
    fcap = max(2, 30 * tiles // (4 * owners) + 1)
    lcap = max(2, 100 * tiles // (4 * owners) + 1)
    share = -(-27 // owners)
    height = fcap * 64 + lcap * 8
    opposite = jnp.array(OPPOSITE, jnp.int32)
    need = jnp.array(line_need(), jnp.int32)
    owner = jnp.concatenate([face_owner.reshape(-1), line_owner.reshape(-1)])
    want = jnp.concatenate([
        (face_slot * 6 + opposite[None, :]).reshape(-1), (line_slot * 12 + need[None, :]).reshape(-1)])
    pos, code = plan(owner, want, owners, tiles * 6, fcap, lcap)
    sent = jnp.broadcast_to(jnp.pad(code, ((0, 0), (0, 128 - fcap - lcap)))[:, None, :], (owners, 8, 128))
    asked = exchange(sent, 3)[:, 0, : fcap + lcap]

    smem = pl.BlockSpec(memory_space=pltpu.SMEM)
    vmem = pl.BlockSpec(memory_space=pltpu.VMEM)
    params = pltpu.CompilerParams(vmem_limit_bytes=56 * 1024 * 1024)
    shape = jax.ShapeDtypeStruct
    table_scratch = [
        pltpu.VMEM((tiles * 6, 8, 8, c), F32),
        pltpu.VMEM((tiles * 12, 8, c), F32),
        pltpu.VMEM((tiles * 6 + 1, 8, 8, c), F32),
        pltpu.VMEM((tiles * 20 + 1, 8, c), F32),
        pltpu.VMEM((12, 10, 8, 4 * c), F32),
        pltpu.VMEM((10, 10, 24, c), F32),
        pltpu.VMEM((12 * c, 3 * c), BF16),
    ]
    got_scratch = [
        pltpu.VMEM((owners * fcap, 8, 8, 2 * c), F32),
        pltpu.VMEM((owners * lcap, 8, 2 * c), F32),
        pltpu.VMEM((tiles * 6, 8, 8, 2 * c), F32),
        pltpu.VMEM((tiles * 12, 8, 2 * c), F32),
        pltpu.VMEM((10, 10, 24, c), F32),
        pltpu.VMEM((10, 10, 8, 4 * c), F32),
        pltpu.VMEM((tiles * 512, 36 * c), BF16),
        pltpu.VMEM((tiles, 8, 8, 8, c), F32),
        pltpu.VMEM((c, 36 * c), BF16),
    ]
    out_block = shape((owners, height, 2 * c), BF16)
    row_block = shape((tiles, 64, 8, c), F32)
    term_block = shape((owners, c, share * c), F32)
    volume = shape(features.shape, BF16)

    outgoing, rows, hidden_own = pl.pallas_call(
        lambda *refs: first_kernel(fcap, *refs),
        out_shape=(out_block, row_block, row_block),
        in_specs=[smem] * 2 + [vmem] * 4,
        out_specs=(vmem,) * 3,
        scratch_shapes=table_scratch,
        compiler_params=params,
    )(asked, code, features, occupancy, cotangent, weight_two)
    arrived = exchange(outgoing, 0)
    outgoing, hidden_rows, feature_own, first_term = pl.pallas_call(
        lambda *refs: second_kernel(fcap, *refs),
        out_shape=(out_block, row_block, row_block, term_block),
        in_specs=[smem] * 3 + [vmem] * 5,
        out_specs=(vmem,) * 4,
        scratch_shapes=table_scratch + got_scratch,
        compiler_params=params,
    )(asked, code, pos, arrived, rows, hidden_own, occupancy, weight_one)
    arrived = exchange(outgoing, 1)
    block_out, feature_grad, second_term = pl.pallas_call(
        lambda *refs: third_kernel(fcap, *refs),
        out_shape=(volume, volume, term_block),
        in_specs=[smem] * 2 + [vmem] * 7,
        out_specs=(vmem,) * 3,
        scratch_shapes=got_scratch,
        compiler_params=params,
    )(asked, pos, arrived, hidden_rows, feature_own, occupancy, features, cotangent, weight_two)
    grad_scale = 1.0 / math.sqrt(512.0 * tiles * owners)
    first_grad, second_grad = reduce_terms(first_term, second_term, grad_scale, 2)
    return (block_out, feature_grad, first_grad, second_grad)


def solution(mesh):
    split = P(("scene", "space", "sub"), None, None)
    split2 = P(("scene", "space", "sub"), None)
    in_specs = (split, split2, split, split2, split, split2, P(), P(), split)
    out_specs = (split, split, P("scene", None, None), P("scene", None, None))
    return jax.shard_map(body, mesh=mesh, in_specs=in_specs, out_specs=out_specs, check_vma=False)
```

```python
import math

import jax
import jax.numpy as jnp
from jax import lax
from jax.experimental import pallas as pl
from jax.experimental.pallas import tpu as pltpu
from jax.sharding import PartitionSpec as P

F32 = jnp.float32
BF16 = jnp.bfloat16
OWNER_AXES = ("space", "sub")

_VECTORS = [(x, y, z) for x in (-1, 0, 1) for y in (-1, 0, 1) for z in (-1, 0, 1)]
EXTRA = [v for v in _VECTORS if sum(c != 0 for c in v) == 2]
EXTRA = EXTRA + [v for v in _VECTORS if sum(c != 0 for c in v) == 3]
OPPOSITE = (1, 0, 3, 2, 5, 4)


def line_need():
    need = []
    for vector in EXTRA:
        zero = [a for a in range(3) if vector[a] == 0]
        main = zero[0] if zero else 2
        rest = [a for a in range(3) if a != main]
        b1 = 0 if vector[rest[0]] > 0 else 1
        b2 = 0 if vector[rest[1]] > 0 else 1
        need.append(main * 4 + b1 * 2 + b2)
    return need


DEAL = [k for k in range(27) if k % 3 < 2] + [k for k in range(27) if k % 3 == 2]


def cut_pieces(values, tile, faces, lines):
    for f in range(6):
        end = 7 * (f % 2)
        if f // 2 == 0:
            piece = values[end]
        elif f // 2 == 1:
            piece = values[:, end]
        else:
            piece = values[:, :, end, :]
        faces[tile * 6 + f] = piece
    for main in range(3):
        for b1 in range(2):
            for b2 in range(2):
                if main == 2:
                    piece = values[7 * b1, 7 * b2]
                elif main == 1:
                    piece = values[7 * b1, :, 7 * b2, :]
                else:
                    piece = values[:, 7 * b1, 7 * b2, :]
                lines[tile * 12 + main * 4 + b1 * 2 + b2] = piece


def conv_back(up_rows, weight, wide, spread, tile, own, grad_faces, grad_lines):
    c = up_rows.shape[-1]
    cube = up_rows.reshape(8, 8, 8, c)
    for j in range(3):
        wide[2:10, j : j + 8, :, j * c : (j + 1) * c] = cube
    total = None
    for kx in range(3):
        cols = wide[2 - kx : 12 - kx].reshape(800, 4 * c).astype(BF16)
        term = jnp.dot(cols, weight[kx * 4 * c : (kx + 1) * 4 * c, :], preferred_element_type=F32)
        total = term if total is None else total + term
    total = total.reshape(10, 10, 8, 3 * c)
    spread[:, :, 16:24, :] = jnp.zeros((10, 10, 8, c), F32)
    spread[:, :, 8:16, :] = total[:, :, :, :c]
    spread[:, :, 9:17, :] += total[:, :, :, c : 2 * c]
    spread[:, :, 10:18, :] += total[:, :, :, 2 * c :]
    own[tile] = spread[1:9, 1:9, 9:17, :].reshape(64, 8, c)
    for f in range(6):
        end = 9 * (f % 2)
        if f // 2 == 0:
            piece = spread[end, 1:9, 9:17, :]
        elif f // 2 == 1:
            piece = spread[1:9, end, 9:17, :]
        else:
            piece = spread[1:9, 1:9, 8 + end, :]
        grad_faces[tile * 6 + f] = piece
    for e, vector in enumerate(EXTRA):
        px, py, pz = [9 if d > 0 else 0 for d in vector]
        if vector[2] == 0:
            piece = spread[px, py, 9:17, :]
        elif vector[1] == 0:
            piece = spread[px, 1:9, 8 + pz, :]
        elif vector[0] == 0:
            piece = spread[1:9, py, 8 + pz, :]
        else:
            row = spread[px, py, 8 + pz : 9 + pz, :]
            spot = 0 if vector[2] > 0 else 7
            at = lax.broadcasted_iota(jnp.int32, (8, c), 0)
            piece = jnp.where(at == spot, jnp.broadcast_to(row, (8, c)), 0.0)
        grad_lines[tile * 20 + e] = piece


def fill_outgoing(asked, code, fcap, out, faces, lines, grad_faces, grad_lines):
    owners, cap = asked.shape
    c = faces.shape[-1]
    no_face, no_line = grad_faces.shape[0] - 1, grad_lines.shape[0] - 1

    def one(d, carry):
        rows = []
        for s in range(cap):
            want = asked[d, s] & 63
            number = code[d, s] >> 6
            if s < fcap:
                fwd = faces[want].reshape(64, c)
                back = grad_faces[jnp.where(number > 0, number - 1, no_face)].reshape(64, c)
            else:
                fwd = lines[want]
                back = grad_lines[jnp.where(number > 0, number - 1 - no_face, no_line)]
            rows.append(jnp.concatenate([fwd, back], axis=1))
        out[d] = jnp.concatenate(rows, axis=0).astype(BF16)
        return carry

    lax.fori_loop(0, owners, one, 0)


def lay_forward(weight, flat):
    c = weight.shape[1]
    for kxy in range(9):
        for kz in range(3):
            lane = (kxy * 4 + kz) * c
            flat[:, lane : lane + c] = weight[kxy * 3 + kz]
        flat[:, (kxy * 4 + 3) * c : (kxy * 4 + 4) * c] = jnp.zeros((c, c), BF16)


def lay_back(weight, flat):
    c = weight.shape[1]
    for kx in range(3):
        for ky in range(3):
            row = (kx * 4 + ky) * c
            for kz in range(3):
                flat[row : row + c, kz * c : (kz + 1) * c] = weight[kx * 9 + ky * 3 + kz]
        flat[(kx * 4 + 3) * c : (kx * 4 + 4) * c, :] = jnp.zeros((c, 3 * c), BF16)


def unpack(arrived, got_faces, got_lines, fcap, lcap):
    owners = arrived.shape[0]

    def one(d, carry):
        block = arrived[d].astype(F32)
        for s in range(fcap):
            got_faces[d * fcap + s] = block[s * 64 : (s + 1) * 64].reshape(8, 8, -1)
        base = fcap * 64
        for s in range(lcap):
            got_lines[d * lcap + s] = block[base + s * 8 : base + (s + 1) * 8]
        return carry

    lax.fori_loop(0, owners, one, 0)


def build_columns(cube, tile, pos, caps, got_faces, got_lines, block, wide, cols):
    c = cube.shape[-1]
    fcap, lcap, face_count = caps
    block[1:9, 1:9, 8:16, :] = cube
    for f in range(6):
        at = pos[tile * 6 + f]
        piece = got_faces[(at >> 8) * fcap + (at & 255)][:, :, :c]
        end = 9 * (f % 2)
        if f // 2 == 0:
            block[end, 1:9, 8:16, :] = piece
        elif f // 2 == 1:
            block[1:9, end, 8:16, :] = piece
        else:
            block[1:9, 1:9, 7 + end, :] = piece
    for e, vector in enumerate(EXTRA):
        at = pos[face_count + tile * 20 + e]
        piece = got_lines[(at >> 8) * lcap + (at & 255)][:, :c]
        px, py, pz = [9 if d > 0 else 0 for d in vector]
        if vector[2] == 0:
            block[px, py, 8:16, :] = piece
        elif vector[1] == 0:
            block[px, 1:9, 7 + pz, :] = piece
        elif vector[0] == 0:
            block[1:9, py, 7 + pz, :] = piece
        else:
            spot = 0 if vector[2] > 0 else 7
            block[px, py, 7 + pz : 8 + pz, :] = piece[spot : spot + 1]
    for kz in range(3):
        wide[:, :, :, kz * c : (kz + 1) * c] = block[:, :, 7 + kz : 15 + kz, :]
    for kxy in range(9):
        kx, ky = kxy // 3, kxy % 3
        window = wide[kx : kx + 8, ky : ky + 8].reshape(512, 4 * c).astype(BF16)
        cols[tile * 512 : (tile + 1) * 512, kxy * 4 * c : (kxy + 1) * 4 * c] = window


def fold_pieces(asked, fcap, got_faces, got_lines, face_sums, line_sums, own, tiles):
    owners = asked.shape[0]
    lcap = asked.shape[1] - fcap
    c = own.shape[-1]
    face_sums[...] = jnp.zeros_like(face_sums)
    line_sums[...] = jnp.zeros_like(line_sums)

    def one(d, carry):
        for s in range(fcap):
            to = asked[d, s] & 63
            face_sums[to] = face_sums[to] + got_faces[d * fcap + s]
        for s in range(lcap):
            to = asked[d, fcap + s] & 63
            line_sums[to] = line_sums[to] + got_lines[d * lcap + s]
        return carry

    lax.fori_loop(0, owners, one, 0)
    for tile in range(tiles):
        for f in range(6):
            piece = face_sums[tile * 6 + f][:, :, c:]
            end = 7 * (f % 2)
            if f // 2 == 0:
                own[tile, end] += piece
            elif f // 2 == 1:
                own[tile, :, end] += piece
            else:
                own[tile, :, :, end, :] += piece
        for main in range(3):
            for b1 in range(2):
                for b2 in range(2):
                    piece = line_sums[tile * 12 + main * 4 + b1 * 2 + b2][:, c:]
                    if main == 2:
                        own[tile, 7 * b1, 7 * b2] += piece
                    elif main == 1:
                        own[tile, 7 * b1, :, 7 * b2, :] += piece
                    else:
                        own[tile, :, 7 * b1, 7 * b2, :] += piece


def deal_term(upstream, cols, terms):
    c = upstream.shape[0]
    term = jnp.dot(upstream, cols[...], preferred_element_type=F32)
    owners = terms.shape[0]
    share = terms.shape[2] // c
    for d in range(owners):
        parts = []
        for k in DEAL[d * share : (d + 1) * share]:
            lane = (k // 3) * 4 * c + (k % 3) * c
            parts.append(term[:, lane : lane + c])
        while len(parts) < share:
            parts.append(jnp.zeros((c, c), F32))
        terms[d] = (parts[0] if share == 1 else jnp.concatenate(parts, axis=1))


def first_kernel(fcap, asked, code, feat, occ, cot, weight, out, rows, own,
                 faces, lines, grad_faces, grad_lines, wide, spread, wb):
    tiles, c = feat.shape[0], feat.shape[1]
    lay_back(weight, wb)
    wide[...] = jnp.zeros_like(wide)
    grad_faces[tiles * 6] = jnp.zeros((8, 8, c), F32)
    grad_lines[tiles * 20] = jnp.zeros((8, c), F32)
    for t in range(tiles):
        live = occ[t : t + 1, :].astype(F32)
        masked = (feat[t].astype(F32) * live).T
        rows[t] = masked.reshape(64, 8, c)
        cut_pieces(masked.reshape(8, 8, 8, c), t, faces, lines)
        upstream = (cot[t].astype(F32) * live).T
        conv_back(upstream, wb, wide, spread, t, own, grad_faces, grad_lines)
    fill_outgoing(asked, code, fcap, out, faces, lines, grad_faces, grad_lines)


def second_kernel(fcap, asked, code, pos, arrived, rows, own_in, occ, weight,
                  out, hidden_rows, own_out, terms,
                  faces, lines, grad_faces, grad_lines, wide_back, spread, wb,
                  got_faces, got_lines, face_sums, line_sums, block, wide, cols, own, wf):
    tiles, c = rows.shape[0], rows.shape[3]
    lcap = asked.shape[1] - fcap
    caps = (fcap, lcap, tiles * 6)
    lay_back(weight, wb)
    lay_forward(weight, wf)
    wide_back[...] = jnp.zeros_like(wide_back)
    wide[:, :, :, 3 * c :] = jnp.zeros((10, 10, 8, c), F32)
    grad_faces[tiles * 6] = jnp.zeros((8, 8, c), F32)
    grad_lines[tiles * 20] = jnp.zeros((8, c), F32)
    unpack(arrived, got_faces, got_lines, fcap, lcap)
    for t in range(tiles):
        own[t] = own_in[t].reshape(8, 8, 8, c)
        build_columns(rows[t].reshape(8, 8, 8, c), t, pos, caps, got_faces, got_lines, block, wide, cols)
    fold_pieces(asked, fcap, got_faces, got_lines, face_sums, line_sums, own, tiles)
    conv = lax.dot_general(wf[...], cols[...], (((1,), (1,)), ((), ())), preferred_element_type=F32)
    grads = []
    for t in range(tiles):
        live = occ[t : t + 1, :].astype(F32)
        pre = live * conv[:, t * 512 : (t + 1) * 512]
        logistic = 1.0 / (1.0 + jnp.exp(-pre))
        hidden = (pre * logistic).astype(BF16).astype(F32).T
        hidden_rows[t] = hidden.reshape(64, 8, c)
        cut_pieces(hidden.reshape(8, 8, 8, c), t, faces, lines)
        grad = own[t].reshape(512, c).T
        act = (grad * live * logistic * (1.0 + pre * (1.0 - logistic))).astype(BF16)
        grads.append(act)
        conv_back(act.astype(F32).T, wb, wide_back, spread, t, own_out, grad_faces, grad_lines)
    fill_outgoing(asked, code, fcap, out, faces, lines, grad_faces, grad_lines)
    deal_term(jnp.concatenate(grads, axis=1), cols, terms)


def third_kernel(fcap, asked, pos, arrived, hidden_rows, own_in, occ, feat, cot, weight,
                 block_out, feature_grad, terms,
                 got_faces, got_lines, face_sums, line_sums, block, wide, cols, own, wf):
    tiles, c = feat.shape[0], feat.shape[1]
    lcap = asked.shape[1] - fcap
    caps = (fcap, lcap, tiles * 6)
    lay_forward(weight, wf)
    wide[:, :, :, 3 * c :] = jnp.zeros((10, 10, 8, c), F32)
    unpack(arrived, got_faces, got_lines, fcap, lcap)
    grads = []
    for t in range(tiles):
        own[t] = own_in[t].reshape(8, 8, 8, c)
        build_columns(hidden_rows[t].reshape(8, 8, 8, c), t, pos, caps, got_faces, got_lines, block, wide, cols)
        grads.append((cot[t].astype(F32) * occ[t : t + 1, :].astype(F32)).astype(BF16))
    deal_term(jnp.concatenate(grads, axis=1), cols, terms)
    conv = lax.dot_general(wf[...], cols[...], (((1,), (1,)), ((), ())), preferred_element_type=F32)
    fold_pieces(asked, fcap, got_faces, got_lines, face_sums, line_sums, own, tiles)
    for t in range(tiles):
        live = occ[t : t + 1, :].astype(F32)
        branch = live * conv[:, t * 512 : (t + 1) * 512]
        block_out[t] = (feat[t].astype(F32) * live + branch).astype(BF16)
        sums = own[t].reshape(512, c).T
        feature_grad[t] = ((cot[t].astype(F32) + sums) * live).astype(BF16)


def remote(src, dst, send, recv, device):
    return pltpu.make_async_remote_copy(
        src_ref=src, dst_ref=dst, send_sem=send, recv_sem=recv,
        device_id=device, device_id_type=pl.DeviceIdType.MESH)


def exchange_kernel(outgoing, arrived, send, recv, local):
    owners = outgoing.shape[0]
    subs = lax.axis_size("sub")
    me = lax.axis_index("space") * subs + lax.axis_index("sub")

    def place(i):
        peer = lax.rem(me + i, owners)
        return peer, {"space": peer // subs, "sub": lax.rem(peer, subs)}

    barrier = pltpu.get_barrier_semaphore()
    for i in range(1, owners):
        pl.semaphore_signal(barrier, inc=1, device_id=place(i)[1], device_id_type=pl.DeviceIdType.MESH)
    own = pltpu.make_async_copy(outgoing.at[me], arrived.at[me], local)
    own.start()
    pl.semaphore_wait(barrier, owners - 1)
    order = sorted(range(1, owners), key=lambda i: abs(i - owners // 2))
    copies = []
    for i in order:
        peer, device = place(i)
        copy = remote(outgoing.at[peer], arrived.at[me], send.at[i], recv.at[i], device)
        copy.start()
        copies.append(copy)
    own.wait()
    for copy in copies:
        copy.wait()


def exchange(outgoing, number):
    owners = outgoing.shape[0]
    place = pl.BlockSpec(memory_space=pltpu.VMEM)
    return pl.pallas_call(
        exchange_kernel,
        out_shape=jax.ShapeDtypeStruct(outgoing.shape, outgoing.dtype),
        in_specs=[place],
        out_specs=place,
        scratch_shapes=[
            pltpu.SemaphoreType.DMA((owners,)),
            pltpu.SemaphoreType.DMA((owners,)),
            pltpu.SemaphoreType.DMA,
        ],
        compiler_params=pltpu.CompilerParams(collective_id=number, has_side_effects=True),
    )(outgoing)


def reduce_kernel(scale, first, second, first_out, second_out, halves, sums, parts, gathered,
                  half_send, half_recv, part_send, part_recv, gather_send, gather_recv,
                  last_send, last_recv):
    spaces, c = sums.shape[0], sums.shape[2]
    space, sub = lax.axis_index("space"), lax.axis_index("sub")
    other = 1 - sub
    partner = {"space": space, "sub": other}

    def peer(i):
        at = lax.rem(space + i, spaces)
        return at, {"space": at, "sub": sub}

    barrier = pltpu.get_barrier_semaphore()
    pl.semaphore_signal(barrier, inc=1, device_id=partner, device_id_type=pl.DeviceIdType.MESH)
    for i in range(1, spaces):
        pl.semaphore_signal(barrier, inc=1, device_id=peer(i)[1], device_id_type=pl.DeviceIdType.MESH)
    pl.semaphore_wait(barrier, spaces)
    order = sorted(range(1, spaces), key=lambda i: abs(i - spaces // 2))
    pieces = []
    for i in order + [0]:
        at = lax.rem(space + i, spaces)
        for j, term in enumerate((first, second)):
            copy = remote(term.at[other * spaces + at], halves.at[j, at],
                          half_send.at[j, i], half_recv.at[j, i], partner)
            copy.start()
            pieces.append(copy)
    copies = []
    for turn, i in enumerate(order + [0]):
        at, device = peer(i)
        for j, term in enumerate((first, second)):
            pieces[2 * turn + j].wait_recv()
            sums[at, j] = (term[sub * spaces + at] + halves[j, at]).astype(BF16)
        if i:
            copy = remote(sums.at[at], parts.at[space], part_send.at[i], part_recv.at[i], device)
            copy.start()
            copies.append(copy)
        else:
            parts[space] = sums[at]
    for copy in pieces:
        copy.wait_send()
    for copy in copies:
        copy.wait()
    total = parts[0].astype(F32)
    for s in range(1, spaces):
        total = total + parts[s].astype(F32)
    gathered[sub, space] = (total * scale).astype(BF16)
    copies = []
    for i in order:
        at, device = peer(i)
        copy = remote(gathered.at[sub, space], gathered.at[sub, space],
                      gather_send.at[i], gather_recv.at[i], device)
        copy.start()
        copies.append(copy)
    lasts = []

    def hand_on(i):
        at = lax.rem(space - i + spaces, spaces)
        copy = remote(gathered.at[sub, at], gathered.at[sub, at], last_send.at[i], last_recv.at[i], partner)
        copy.start()
        lasts.append(copy)

    hand_on(0)
    for i, copy in reversed(list(zip(order, copies))):
        copy.wait_recv()
        hand_on(i)
    for copy in copies:
        copy.wait_send()
    for copy in lasts:
        copy.wait()
    share = gathered.shape[4] // c
    for at, k in enumerate(DEAL):
        owner, lane = at // share, at % share * c
        for j, out in enumerate((first_out, second_out)):
            out[k] = gathered[owner // spaces, owner % spaces, j][:, lane : lane + c].astype(F32)


def reduce_terms(first, second, scale, number):
    subs, spaces = lax.axis_size("sub"), lax.axis_size("space")
    owners, c, width = first.shape
    vmem = pl.BlockSpec(memory_space=pltpu.VMEM)
    dma = pltpu.SemaphoreType.DMA
    return pl.pallas_call(
        lambda *refs: reduce_kernel(scale, *refs),
        out_shape=(jax.ShapeDtypeStruct((27, c, c), F32),) * 2,
        in_specs=[vmem] * 2,
        out_specs=(vmem,) * 2,
        scratch_shapes=[
            pltpu.VMEM((2, spaces, c, width), F32),
            pltpu.VMEM((spaces, 2, c, width), BF16),
            pltpu.VMEM((spaces, 2, c, width), BF16),
            pltpu.VMEM((subs, spaces, 2, c, width), BF16),
            dma((2, spaces)), dma((2, spaces)), dma((spaces,)), dma((spaces,)),
            dma((spaces,)), dma((spaces,)), dma((spaces,)), dma((spaces,)),
        ],
        compiler_params=pltpu.CompilerParams(
            collective_id=number, has_side_effects=True, vmem_limit_bytes=32 * 1024 * 1024),
    )(first, second)


def plan(owner, want, owners, faces, fcap, lcap):
    count = owner.shape[0]
    cap = fcap + lcap
    at = jnp.arange(count, dtype=jnp.int32)
    line = (at >= faces).astype(jnp.int32)
    group = owner * 2 + line
    earlier = (at[None, :] < at[:, None]) & (group[None, :] == group[:, None])
    rank = jnp.sum(earlier.astype(jnp.int32), axis=1)
    slot = owner * cap + line * fcap + rank
    hit = slot[None, :] == jnp.arange(owners * cap, dtype=jnp.int32)[:, None]
    code = jnp.sum(jnp.where(hit, (at * 64 + 64 + want)[None, :], 0), axis=1)
    return owner * 256 + rank, code.reshape(owners, cap)


def body(features, occupancy, face_owner, face_slot, line_owner, line_slot, weight_one, weight_two, cotangent):
    owners = lax.axis_size(OWNER_AXES)
    tiles, c = features.shape[0], features.shape[1]
    fcap = max(2, 30 * tiles // (4 * owners) + 1)
    lcap = max(2, 100 * tiles // (4 * owners) + 1)
    share = -(-27 // owners)
    height = fcap * 64 + lcap * 8
    opposite = jnp.array(OPPOSITE, jnp.int32)
    need = jnp.array(line_need(), jnp.int32)
    owner = jnp.concatenate([face_owner.reshape(-1), line_owner.reshape(-1)])
    want = jnp.concatenate([
        (face_slot * 6 + opposite[None, :]).reshape(-1), (line_slot * 12 + need[None, :]).reshape(-1)])
    pos, code = plan(owner, want, owners, tiles * 6, fcap, lcap)
    sent = jnp.broadcast_to(jnp.pad(code, ((0, 0), (0, 128 - fcap - lcap)))[:, None, :], (owners, 8, 128))
    asked = exchange(sent, 3)[:, 0, : fcap + lcap]

    smem = pl.BlockSpec(memory_space=pltpu.SMEM)
    vmem = pl.BlockSpec(memory_space=pltpu.VMEM)
    params = pltpu.CompilerParams(vmem_limit_bytes=56 * 1024 * 1024)
    shape = jax.ShapeDtypeStruct
    table_scratch = [
        pltpu.VMEM((tiles * 6, 8, 8, c), F32),
        pltpu.VMEM((tiles * 12, 8, c), F32),
        pltpu.VMEM((tiles * 6 + 1, 8, 8, c), F32),
        pltpu.VMEM((tiles * 20 + 1, 8, c), F32),
        pltpu.VMEM((12, 10, 8, 4 * c), F32),
        pltpu.VMEM((10, 10, 24, c), F32),
        pltpu.VMEM((12 * c, 3 * c), BF16),
    ]
    got_scratch = [
        pltpu.VMEM((owners * fcap, 8, 8, 2 * c), F32),
        pltpu.VMEM((owners * lcap, 8, 2 * c), F32),
        pltpu.VMEM((tiles * 6, 8, 8, 2 * c), F32),
        pltpu.VMEM((tiles * 12, 8, 2 * c), F32),
        pltpu.VMEM((10, 10, 24, c), F32),
        pltpu.VMEM((10, 10, 8, 4 * c), F32),
        pltpu.VMEM((tiles * 512, 36 * c), BF16),
        pltpu.VMEM((tiles, 8, 8, 8, c), F32),
        pltpu.VMEM((c, 36 * c), BF16),
    ]
    out_block = shape((owners, height, 2 * c), BF16)
    row_block = shape((tiles, 64, 8, c), F32)
    term_block = shape((owners, c, share * c), F32)
    volume = shape(features.shape, BF16)

    outgoing, rows, hidden_own = pl.pallas_call(
        lambda *refs: first_kernel(fcap, *refs),
        out_shape=(out_block, row_block, row_block),
        in_specs=[smem] * 2 + [vmem] * 4,
        out_specs=(vmem,) * 3,
        scratch_shapes=table_scratch,
        compiler_params=params,
    )(asked, code, features, occupancy, cotangent, weight_two)
    arrived = exchange(outgoing, 0)
    outgoing, hidden_rows, feature_own, first_term = pl.pallas_call(
        lambda *refs: second_kernel(fcap, *refs),
        out_shape=(out_block, row_block, row_block, term_block),
        in_specs=[smem] * 3 + [vmem] * 5,
        out_specs=(vmem,) * 4,
        scratch_shapes=table_scratch + got_scratch,
        compiler_params=params,
    )(asked, code, pos, arrived, rows, hidden_own, occupancy, weight_one)
    arrived = exchange(outgoing, 1)
    block_out, feature_grad, second_term = pl.pallas_call(
        lambda *refs: third_kernel(fcap, *refs),
        out_shape=(volume, volume, term_block),
        in_specs=[smem] * 2 + [vmem] * 7,
        out_specs=(vmem,) * 3,
        scratch_shapes=got_scratch,
        compiler_params=params,
    )(asked, pos, arrived, hidden_rows, feature_own, occupancy, features, cotangent, weight_two)
    grad_scale = 1.0 / math.sqrt(512.0 * tiles * owners)
    first_grad, second_grad = reduce_terms(first_term, second_term, grad_scale, 2)
    return (block_out, feature_grad, first_grad, second_grad)


def solution(mesh):
    split = P(("scene", "space", "sub"), None, None)
    split2 = P(("scene", "space", "sub"), None)
    in_specs = (split, split2, split, split2, split, split2, P(), P(), split)
    out_specs = (split, split, P("scene", None, None), P("scene", None, None))
    return jax.shard_map(body, mesh=mesh, in_specs=in_specs, out_specs=out_specs, check_vma=False)
```
